32 devices in a mesh: shard: 2 (over y), loop: 16 (over z, x, core).
Axes of the slice: x: 2, y: 2, z: 4, core: 2. Of those that a mesh axis runs over, the one named last changes fastest.
Arguments:
- hidden: bfloat16 [61440, 768], P(('shard', 'loop')), may hold values from -6 to 6
- segment: int32 [61440], P(('shard', 'loop')), may hold values from 0 to 8, as said below
- counts: int32 [256], P(('shard', 'loop')), may hold values from 1 to 720, as said below
- w_proj: bfloat16 [768, 128], replicated, may hold values from -0.21875 to 0.21875
- seeds: bfloat16 [256, 32, 128], P('loop', 'shard'), may hold values from -6 to 6
Outputs:
- scores: float32 [256, 256], P(('shard', 'loop'))
The draws below stay inside these ranges and needn't reach their ends.
Inputs may be any that keep to these rules, and one draw needn't show every extreme that they name: On every device one document has exactly 720 tokens, and a device's counts sum to less than 1920. `segment`: within a device, document k occupies counts of that document consecutive slots, documents in order of k from the first slot; all later slots hold 8, and every device has at least one such slot.
All inputs are finite; a program needn't handle non-finite values.
Results may differ from the reference program's by a relative error of at most 0.00055.
Values may be sent and summed in bfloat16 or wider, within the bound.
No kernel may reach another device: no remote copies, remote signals or barrier semaphores. Data moves between devices by JAX's collectives and lax.ppermute only.
A program may use at most 64 MiB of HBM per device.

```python
import jax
import jax.numpy as jnp
from jax import lax

D_IN = 768
D = 128
QT = 32
Q = 256
MAXLEN = 720
DOC_DEV = 8
ROWS_DEV = 1920
DOCS = 256
ROWS = 61440
N_LOOP = 16


def length_table(key):
    device_count = DOCS // DOC_DEV
    others = min(MAXLEN, (ROWS_DEV - MAXLEN - 1) // (DOC_DEV - 1))
    base = jax.random.randint(jax.random.fold_in(key, 11), (device_count, DOC_DEV), 1, others + 1)
    chosen = jax.random.randint(jax.random.fold_in(key, 12), (device_count,), 0, DOC_DEV)
    slots = jnp.arange(DOC_DEV, dtype=jnp.int32)[None, :]
    return jnp.where(slots == chosen[:, None], MAXLEN, base).astype(jnp.int32)


def draw_counts(key, part):
    return length_table(key).reshape(DOCS)


def draw_segment(key, part):
    table = length_table(key)
    ends = jnp.cumsum(table, axis=1)
    places = jnp.arange(ROWS_DEV, dtype=jnp.int32)
    labels = jnp.sum((places[None, :, None] >= ends[:, None, :]).astype(jnp.int32), axis=-1)
    return labels.reshape(ROWS).astype(jnp.int32)


def steps_of(own_key, dims, cuts, low, high):
    gain, own = 1.0, jax.random.fold_in(own_key, 6)
    for dim, parts in cuts:
        steps = jnp.exp(jax.random.uniform(jax.random.fold_in(own, dim), (parts,), jnp.float32, low / len(cuts), high / len(cuts)))
        gain = gain * jnp.repeat(steps, dims[dim] // parts).reshape([-1 if axis == dim else 1 for axis in range(len(dims))])
    return gain


def scatter_about(rng, extent, deviation, limit, cuts=(), kind=jnp.bfloat16):
    values = jax.random.normal(rng, extent, jnp.float32) * deviation
    if len(cuts) > 0:
        values = steps_of(rng, extent, cuts, -0.22, 0.18) * values
    return jnp.clip(values, min=-limit, max=limit).astype(kind)


def setup_inputs(seed: int = 0) -> dict:
    keys = jax.random.split(jax.random.key(seed), 6)
    hidden = scatter_about(keys[0], (ROWS, D_IN), 1.0, 6.0, ((0, 32),))
    segment = draw_segment(jax.random.fold_in(keys[5], 71), 0)
    counts = draw_counts(jax.random.fold_in(keys[5], 71), 0)
    w_proj = scatter_about(keys[3], (D_IN, D), D_IN ** -0.5, 0.21875)
    seeds = scatter_about(keys[4], (Q, QT, D), 1.0, 6.0, ((0, 16), (1, 2)))
    return {"hidden": hidden, "segment": segment, "counts": counts, "w_proj": w_proj, "seeds": seeds}


BETA = 16.0
EPS = 1e-06

def unit_rows(values):
    values = values.astype(jnp.float32)
    return (values * lax.rsqrt(lax.optimization_barrier(jnp.sum(values * values, axis=-1, keepdims=True)) + EPS)).astype(jnp.bfloat16)

def reference(hidden, segment, counts, w_proj, seeds):
    projected = jnp.dot(hidden, w_proj, preferred_element_type=jnp.float32)
    doc_vectors = unit_rows(projected)
    seed_vectors = unit_rows(seeds)
    device_count = DOCS // DOC_DEV
    group = Q // N_LOOP
    blocks = seed_vectors.reshape(N_LOOP, group * QT, D)
    vectors = doc_vectors.reshape(device_count, ROWS_DEV, D)
    labels = segment.reshape(device_count, ROWS_DEV).astype(jnp.int32)
    sizes = counts.reshape(device_count, DOC_DEV).astype(jnp.float32)

    def one_device(item):
        rows, ids, lengths = item

        def one_block(block):
            sims = jnp.dot(rows, block.T, preferred_element_type=jnp.float32)
            mass = jax.ops.segment_sum(jnp.exp(BETA * sims), ids, num_segments=DOC_DEV + 1)[:DOC_DEV]
            logs = jnp.log(mass / lengths[:, None]).reshape(DOC_DEV, group, QT)
            return lax.optimization_barrier(jnp.mean(logs, axis=-1))
        result = lax.map(one_block, blocks)
        return jnp.transpose(result, (1, 0, 2)).reshape(DOC_DEV, Q)
    result = lax.map(one_device, (vectors, labels, sizes))
    return result.reshape(DOCS, Q)
```

```python
import functools

import jax
import jax.numpy as jnp
from jax import lax
from jax.experimental import pallas as pl
from jax.experimental.pallas import tpu as pltpu
from jax.sharding import PartitionSpec as P

BETA = 16.0
EPS = 1e-06
LOG2E = 1.4426950408889634
GROUP = 16
PIECE = 256
SMEM = pl.BlockSpec(memory_space=pltpu.SMEM)
VMEM = pl.BlockSpec(memory_space=pltpu.VMEM)


def unit_rows(values):
    values = values.astype(jnp.float32)
    return (values * lax.rsqrt(jnp.sum(values * values, axis=-1, keepdims=True) + EPS)).astype(
        jnp.bfloat16
    )


def params(mib):
    return pltpu.CompilerParams(vmem_limit_bytes=mib * 2**20)


def docs_kernel(counts, hidden, w_proj, rows_out, slot, keep, vectors):
    docs = counts.shape[0]
    rows = hidden.shape[0]
    groups = slot.shape[0]
    step = 384 if rows % 384 == 0 else rows
    for lo in range(0, rows, step):
        projected = jnp.dot(
            hidden[lo : lo + step, :], w_proj[...], preferred_element_type=jnp.float32
        )
        vectors[lo : lo + step, :] = unit_rows(projected).astype(jnp.float32)
    vectors[rows:, :] = jnp.zeros_like(vectors[rows:, :])
    tail = docs * GROUP
    rows_out[tail:, :] = jnp.zeros_like(rows_out[tail:, :])

    def fill(g, carry):
        slot[g] = docs
        keep[g] = 0.0
        return carry

    lax.fori_loop(0, groups, fill, 0, unroll=8)
    start = jnp.int32(0)
    first = jnp.int32(0)
    for d in range(docs):
        count = counts[d]
        full = count // GROUP

        def move(k, carry, d=d, start=start, first=first):
            g = first + k
            block = vectors[pl.ds(start + k * GROUP, GROUP), :]
            rows_out[pl.ds(pl.multiple_of(tail + g * GROUP, GROUP), GROUP), :] = block.astype(
                jnp.bfloat16
            )
            slot[g] = d
            keep[g] = jnp.where(k == 0, 0.0, 1.0)
            return carry

        lax.fori_loop(0, full, move, 0)
        block = vectors[pl.ds(start + full * GROUP, GROUP), :]
        rows_out[d * GROUP : (d + 1) * GROUP, :] = block.astype(jnp.bfloat16)
        start = start + count
        first = first + full


def regroup_documents(hidden, counts, w_proj):
    rows, docs = hidden.shape[0], counts.shape[0]
    width = w_proj.shape[1]
    groups = rows // GROUP
    return pl.pallas_call(
        docs_kernel,
        out_shape=(
            jax.ShapeDtypeStruct((docs * GROUP + rows, width), jnp.bfloat16),
            jax.ShapeDtypeStruct((groups,), jnp.int32),
            jax.ShapeDtypeStruct((groups,), jnp.float32),
        ),
        in_specs=[SMEM, VMEM, VMEM],
        out_specs=(VMEM, SMEM, SMEM),
        scratch_shapes=[pltpu.VMEM((rows + GROUP, width), jnp.float32)],
        compiler_params=params(16),
        name="documents",
    )(counts, hidden, w_proj)


def unit_kernel(*refs):
    *pieces, out = refs
    for i, piece in enumerate(pieces):
        values = piece[...].reshape(PIECE, piece.shape[-1])
        out[i * PIECE : (i + 1) * PIECE, :] = unit_rows(values)


def unit_pieces(*pieces):
    return pl.pallas_call(
        unit_kernel,
        out_shape=jax.ShapeDtypeStruct((len(pieces) * PIECE, pieces[0].shape[-1]), jnp.bfloat16),
        in_specs=[VMEM] * len(pieces),
        out_specs=VMEM,
        compiler_params=params(8),
        name="unit_pieces",
    )(*pieces)


def mass_kernel(places, counts, slot, keep, rows, *refs):
    *chunks, mass, open_sums, tail_sums = refs
    chunks = chunks[-len(places) :]
    docs = counts.shape[0]
    groups = slot.shape[0]
    tail = docs * GROUP

    def weights(block, tokens):
        sims = lax.dot_general(
            block, tokens, (((1,), (1,)), ((), ())), preferred_element_type=jnp.float32
        )
        return jnp.exp2(sims * (BETA * LOG2E))

    for chunk, place in zip(chunks, places):
        tokens = chunk[...]
        wide = tokens.shape[0]
        open_sums[...] = jnp.zeros_like(open_sums)
        block = weights(rows[:tail, :], tokens)
        place8 = lax.broadcasted_iota(jnp.int32, (GROUP // 2, wide), 0)
        for d in range(docs):
            left = counts[d] % GROUP
            lo = d * GROUP
            mid, hi = lo + GROUP // 2, lo + GROUP
            tail_sums[d] = jnp.where(place8 < left, block[lo:mid], 0.0) + jnp.where(
                place8 + GROUP // 2 < left, block[mid:hi], 0.0
            )
        total = jnp.zeros((GROUP // 2, wide), jnp.float32)
        step = 32 if groups % 32 == 0 else 24 if groups % 24 == 0 else groups
        for base in range(0, groups, step):
            block = weights(rows[tail + base * GROUP : tail + (base + step) * GROUP, :], tokens)
            for j in range(step):
                lo = j * GROUP
                mid, hi = lo + GROUP // 2, lo + GROUP
                total = total * keep[base + j] + (block[lo:mid] + block[mid:hi])
                open_sums[slot[base + j]] = total
        sums = jnp.sum(open_sums[:docs] + tail_sums[...], axis=1)
        for i, at in enumerate(place):
            mass[at] = sums[:, i * PIECE : (i + 1) * PIECE]


def add_masses(counts, slot, keep, rows, mass, chunks, places, pieces):
    docs = counts.shape[0]
    wide = chunks[0].shape[0]
    half = GROUP // 2
    before = () if mass is None else (mass,)
    return pl.pallas_call(
        functools.partial(mass_kernel, places),
        out_shape=jax.ShapeDtypeStruct((pieces, docs, PIECE), jnp.float32),
        in_specs=[SMEM, SMEM, SMEM] + [VMEM] * (1 + len(before) + len(chunks)),
        out_specs=VMEM,
        input_output_aliases={4: 0} if before else {},
        scratch_shapes=[
            pltpu.VMEM((docs + 1, half, wide), jnp.float32),
            pltpu.VMEM((docs, half, wide), jnp.float32),
        ],
        compiler_params=params(24),
        name="masses",
    )(counts, slot, keep, rows, *before, *chunks)


def score_kernel(parts, tokens, own, counts, mass, scores):
    pieces, docs, _ = mass.shape
    groups = pieces // parts
    queries = PIECE // tokens
    per_tile = 128 // queries
    lengths = jnp.concatenate(
        [jnp.full((1, PIECE), counts[d].astype(jnp.float32)) for d in range(docs)], axis=0
    )
    logs = []
    for group in range(groups):
        relative = group ^ own[0]
        total = jnp.log(mass[relative * parts] / lengths)
        for part in range(1, parts):
            total = total + jnp.log(mass[relative * parts + part] / lengths)
        logs.append(total)
    place = lax.broadcasted_iota(jnp.int32, (PIECE, 128), 0) // tokens
    column = lax.broadcasted_iota(jnp.int32, (PIECE, 128), 1)
    tiles = groups // per_tile
    total = jnp.zeros((tiles * docs, 128), jnp.float32)
    for i in range(per_tile):
        pick = (column == place + i * queries).astype(jnp.bfloat16)
        rest = jnp.concatenate([logs[tile * per_tile + i] for tile in range(tiles)], axis=0)
        for _ in range(3):
            head = rest.astype(jnp.bfloat16)
            total = total + jnp.dot(head, pick, preferred_element_type=jnp.float32)
            rest = rest - head.astype(jnp.float32)
    total = total * (1.0 / (tokens * parts))
    for tile in range(tiles):
        scores[:, tile * 128 : (tile + 1) * 128] = total[tile * docs : (tile + 1) * docs]


def score(parts, tokens, own, counts, mass):
    pieces, docs, _ = mass.shape
    queries = pieces // parts * (PIECE // tokens)
    return pl.pallas_call(
        functools.partial(score_kernel, parts, tokens),
        out_shape=jax.ShapeDtypeStruct((docs, queries), jnp.float32),
        in_specs=[SMEM, SMEM, VMEM],
        out_specs=VMEM,
        compiler_params=params(8),
        name="scores",
    )(own, counts, mass)


def swap(values, mask, devices):
    return lax.ppermute(values, ("shard", "loop"), [(i, i ^ mask) for i in range(devices)])


def pair_body(hidden, segment, counts, w_proj, seeds):
    devices = 32
    core, x, z, far, y = 1, 2, 4, 8, 16
    send = functools.partial(swap, devices=devices)
    raw = [seeds, send(seeds, z), send(seeds, far), send(seeds, z | far)]
    rows, slot, keep = regroup_documents(hidden, counts, w_proj)
    own = unit_pieces(*raw)
    a, b = own[: 2 * PIECE], own[2 * PIECE :]
    ax, by = send(a, x), send(b, y)
    ay, bx = send(a, y), send(b, x)
    axy, byx = send(ax, y), send(by, x)
    mass = None
    for va, vb, ma, mb in (
        (a, b, 0, 0),
        (ax, by, x, y),
        (ay, bx, y, x),
        (axy, byx, x | y, x | y),
    ):
        places = (pair_places(ma, 0, z), pair_places(mb, far, z | far))
        mass = add_masses(counts, slot, keep, rows, mass, (va, vb), places, devices)
        places = (pair_places(ma | core, 0, z), pair_places(mb | core, far, z | far))
        chunks = (send(va, core), send(vb, core))
        mass = add_masses(counts, slot, keep, rows, mass, chunks, places, devices)
    mine = lax.axis_index("loop").astype(jnp.int32).reshape(1)
    return score(2, 16, mine, counts, mass)


def pair_places(mask, *along_z):
    return tuple(((mask & 15) ^ bits) * 2 + (mask >> 4) for bits in along_z)


def whole_body(hidden, segment, counts, w_proj, seeds):
    own = lax.all_gather(unit_rows(seeds), "shard", axis=1, tiled=True)
    every = lax.all_gather(own, "loop", axis=0, tiled=True)
    tokens = every.shape[1]
    every = every.reshape(-1, every.shape[-1])
    pieces = every.shape[0] // PIECE
    rows, slot, keep = regroup_documents(hidden, counts, w_proj)
    mass = None
    for first in range(0, pieces, 4):
        chunks = tuple(every[i * PIECE : (i + 2) * PIECE] for i in (first, first + 2))
        places = ((first, first + 1), (first + 2, first + 3))
        mass = add_masses(counts, slot, keep, rows, mass, chunks, places, pieces)
    return score(1, tokens, jnp.zeros((1,), jnp.int32), counts, mass)


def solution(mesh):
    in_specs = (
        P(("shard", "loop"), None),
        P(("shard", "loop")),
        P(("shard", "loop")),
        P(),
        P("loop", "shard", None),
    )
    out_specs = P(("shard", "loop"), None)
    paired = mesh.shape["shard"] == 2 and mesh.shape["loop"] == 16
    body = pair_body if paired else whole_body
    return jax.shard_map(body, mesh=mesh, in_specs=in_specs, out_specs=out_specs, check_vma=False)
```

```python
import functools

import jax
import jax.numpy as jnp
from jax import lax
from jax.experimental import pallas as pl
from jax.experimental.pallas import tpu as pltpu
from jax.sharding import PartitionSpec as P

BETA = 16.0
EPS = 1e-06
LOG2E = 1.4426950408889634
GROUP = 16
HALF = GROUP // 2
PIECE = 256
LANES = 128
ANY = pl.BlockSpec(memory_space=pl.ANY)
VMEM = pl.BlockSpec(memory_space=pltpu.VMEM)


def unit_rows(values):
    values = values.astype(jnp.float32)
    return (values * lax.rsqrt(jnp.sum(values * values, axis=-1, keepdims=True) + EPS)).astype(
        jnp.bfloat16
    )


def params(mib):
    return pltpu.CompilerParams(vmem_limit_bytes=mib * 2**20)


def cost(micros):
    return pl.CostEstimate(flops=int(micros * 1e9), bytes_accessed=0, transcendentals=0)


def docs_kernel(counts_hbm, hidden, w_proj, rows_out, inside, keep, last, lengths, vectors, counts, sem):
    docs = last.shape[0]
    rows = hidden.shape[0]
    groups = rows // GROUP
    tail = docs * GROUP
    fetch = pltpu.make_async_copy(counts_hbm, counts, sem)
    fetch.start()
    step = 384 if rows % 384 == 0 else rows
    for lo in range(0, rows, step):
        projected = jnp.dot(
            hidden[lo : lo + step, :], w_proj[...], preferred_element_type=jnp.float32
        )
        vectors[lo : lo + step, :] = unit_rows(projected).astype(jnp.float32)
    vectors[rows:, :] = jnp.zeros_like(vectors[rows:, :])
    rows_out[tail:, :] = jnp.zeros_like(rows_out[tail:, :])
    fetch.wait()
    group = lax.broadcasted_iota(jnp.int32, keep.shape, 0)
    document = lax.broadcasted_iota(jnp.int32, last.shape, 0)
    place = lax.broadcasted_iota(jnp.int32, (GROUP, LANES), 0)
    keeps = jnp.ones(keep.shape, jnp.float32)
    lasts = jnp.zeros(last.shape, jnp.int32)
    sizes = jnp.zeros(last.shape, jnp.float32)
    start = jnp.int32(0)
    first = jnp.int32(0)
    for d in range(docs):
        count = counts[d]
        full = count // GROUP

        def move(k, carry, start=start, first=first):
            block = vectors[pl.ds(start + k * GROUP, GROUP), :]
            at = pl.multiple_of(tail + (first + k) * GROUP, GROUP)
            rows_out[pl.ds(at, GROUP), :] = block.astype(jnp.bfloat16)
            return carry

        lax.fori_loop(0, full, move, 0)
        block = vectors[pl.ds(start + full * GROUP, GROUP), :]
        rows_out[d * GROUP : (d + 1) * GROUP, :] = block.astype(jnp.bfloat16)
        inside[d * GROUP : (d + 1) * GROUP, :] = (place < count - full * GROUP).astype(jnp.float32)
        keeps = jnp.where(group == jnp.where(full > 0, first, groups), 0.0, keeps)
        lasts = jnp.where(document == d, jnp.where(full > 0, first + full - 1, groups), lasts)
        sizes = jnp.where(document == d, count.astype(jnp.float32), sizes)
        start = start + count
        first = first + full
    keep[...] = keeps
    last[...] = lasts
    lengths[...] = sizes


def regroup_documents(hidden, counts, w_proj):
    rows, docs = hidden.shape[0], counts.shape[0]
    width = w_proj.shape[1]
    groups = rows // GROUP
    return pl.pallas_call(
        docs_kernel,
        out_shape=(
            jax.ShapeDtypeStruct((docs * GROUP + rows, width), jnp.bfloat16),
            jax.ShapeDtypeStruct((docs * GROUP, LANES), jnp.float32),
            jax.ShapeDtypeStruct((groups, LANES), jnp.float32),
            jax.ShapeDtypeStruct((docs, LANES), jnp.int32),
            jax.ShapeDtypeStruct((docs, LANES), jnp.float32),
        ),
        in_specs=[ANY, VMEM, VMEM],
        out_specs=(VMEM,) * 5,
        scratch_shapes=[
            pltpu.VMEM((rows + GROUP, width), jnp.float32),
            pltpu.SMEM((docs,), jnp.int32),
            pltpu.SemaphoreType.DMA,
        ],
        compiler_params=params(16),
        cost_estimate=cost(3),
        name="documents",
    )(counts, hidden, w_proj)


def unit_kernel(*refs):
    *pieces, out = refs
    for i, piece in enumerate(pieces):
        values = piece[...].reshape(PIECE, piece.shape[-1])
        out[i * PIECE : (i + 1) * PIECE, :] = unit_rows(values)


def unit_pieces(*pieces):
    return pl.pallas_call(
        unit_kernel,
        out_shape=jax.ShapeDtypeStruct((len(pieces) * PIECE, pieces[0].shape[-1]), jnp.bfloat16),
        in_specs=[VMEM] * len(pieces),
        out_specs=VMEM,
        compiler_params=params(8),
        cost_estimate=cost(0.2),
        name="unit_pieces",
    )(*pieces)


def mass_kernel(places, rows, inside, keep, last, *refs):
    *chunks, mass, sums, tail_sums = refs
    chunks = chunks[-len(places) :]
    docs = last.shape[0]
    groups = keep.shape[0]
    tail = docs * GROUP

    def weights(block, tokens):
        sims = lax.dot_general(
            block, tokens, (((1,), (1,)), ((), ())), preferred_element_type=jnp.float32
        )
        return jnp.exp2(sims * (BETA * LOG2E))

    def wide(row, width):
        return jnp.concatenate([row] * (width // LANES), axis=1)

    step = 24 if groups % 24 == 0 else groups
    ends = last[...]
    for c, (chunk, place) in enumerate(zip(chunks, places)):
        tokens = chunk[...]
        width = tokens.shape[0]
        block = weights(rows[:tail, :], tokens)
        for d in range(docs):
            lo = d * GROUP
            mid, hi = lo + HALF, lo + GROUP
            tail_sums[c, d] = block[lo:mid] * wide(inside[lo:mid, :], width) + block[
                mid:hi
            ] * wide(inside[mid:hi, :], width)
        total = jnp.zeros((HALF, width), jnp.float32)
        sums[c, groups] = total
        for base in range(0, groups, step):
            block = weights(rows[tail + base * GROUP : tail + (base + step) * GROUP, :], tokens)
            for j in range(step):
                lo = j * GROUP
                mid, hi = lo + HALF, lo + GROUP
                row = jnp.broadcast_to(keep[base + j : base + j + 1, :], (HALF, LANES))
                total = total * wide(row, width) + (block[lo:mid] + block[mid:hi])
                sums[c, base + j] = total
    for c, (chunk, place) in enumerate(zip(chunks, places)):
        for d in range(docs):
            total = jnp.sum(sums[c, ends[d, 0]] + tail_sums[c, d], axis=0, keepdims=True)
            for i, at in enumerate(place):
                mass[at, d : d + 1, :] = total[:, i * PIECE : (i + 1) * PIECE]


def add_masses(documents, mass, chunks, places, pieces):
    rows, inside, keep, last, _ = documents
    docs, groups = last.shape[0], keep.shape[0]
    count, width = len(chunks), chunks[0].shape[0]
    before = () if mass is None else (mass,)
    return pl.pallas_call(
        functools.partial(mass_kernel, places),
        out_shape=jax.ShapeDtypeStruct((pieces, docs, PIECE), jnp.float32),
        in_specs=[VMEM] * (4 + len(before) + count),
        out_specs=VMEM,
        input_output_aliases={4: 0} if before else {},
        scratch_shapes=[
            pltpu.VMEM((count, groups + 1, HALF, width), jnp.float32),
            pltpu.VMEM((count, docs, HALF, width), jnp.float32),
        ],
        compiler_params=params(28),
        cost_estimate=cost(1.2 * count * width / 1024),
        name="masses",
    )(rows, inside, keep, last, *before, *chunks)


def score_kernel(parts, tokens, relative, lengths, mass, scores):
    pieces, docs, _ = mass.shape
    groups = pieces // parts
    queries = PIECE // tokens
    per_tile = LANES // queries
    tiles = groups // per_tile
    own = lax.axis_index("loop") if relative else 0
    sizes = jnp.concatenate([lengths[...]] * (PIECE // LANES), axis=1)
    place = lax.broadcasted_iota(jnp.int32, (PIECE, LANES), 0) // tokens
    column = lax.broadcasted_iota(jnp.int32, (PIECE, LANES), 1)
    total = jnp.zeros((tiles * docs, LANES), jnp.float32)
    for i in range(per_tile):
        logs = []
        for tile in range(tiles):
            at = ((tile * per_tile + i) ^ own) * parts
            logs.append(sum(jnp.log(mass[at + part] / sizes) for part in range(parts)))
        rest = jnp.concatenate(logs, axis=0)
        pick = (column == place + i * queries).astype(jnp.bfloat16)
        for _ in range(3):
            head = rest.astype(jnp.bfloat16)
            total = total + jnp.dot(head, pick, preferred_element_type=jnp.float32)
            rest = rest - head.astype(jnp.float32)
    total = total * (1.0 / (tokens * parts))
    for tile in range(tiles):
        scores[:, tile * LANES : (tile + 1) * LANES] = total[tile * docs : (tile + 1) * docs]


def score(parts, tokens, relative, lengths, mass):
    pieces, docs, _ = mass.shape
    queries = pieces // parts * (PIECE // tokens)
    return pl.pallas_call(
        functools.partial(score_kernel, parts, tokens, relative),
        out_shape=jax.ShapeDtypeStruct((docs, queries), jnp.float32),
        in_specs=[VMEM, VMEM],
        out_specs=VMEM,
        compiler_params=params(8),
        cost_estimate=cost(1),
        name="scores",
    )(lengths, mass)


def swap(values, mask, devices):
    return lax.ppermute(values, ("shard", "loop"), [(i, i ^ mask) for i in range(devices)])


def pair_places(mask, *along_z):
    return tuple(((mask & 15) ^ bits) * 2 + (mask >> 4) for bits in along_z)


def pair_body(hidden, segment, counts, w_proj, seeds):
    devices = 32
    core, x, z, far, y = 1, 2, 4, 8, 16
    near, away = (0, z), (far, z | far)
    send = functools.partial(swap, devices=devices)
    raw_far = send(seeds, far)
    raw_z = send(seeds, z)
    documents = regroup_documents(hidden, counts, w_proj)
    a = unit_pieces(seeds, raw_z)
    raw_both = send(raw_far, z)
    ax, ay = send(a, x), send(a, y)
    b = unit_pieces(raw_far, raw_both)
    bx, by = send(b, x), send(b, y)
    axy, byx = send(ax, y), send(by, x)
    mass = None
    for va, vb, ma, mb, za, zb in (
        (a, b, 0, 0, near, away),
        (ax, ay, x, y, near, near),
        (bx, by, x, y, away, away),
        (axy, byx, x | y, x | y, near, away),
    ):
        places = (pair_places(ma, *za), pair_places(mb, *zb))
        mass = add_masses(documents, mass, (va, vb), places, devices)
        other = send(jnp.concatenate([va, vb], axis=0), core)
        places = (pair_places(ma | core, *za) + pair_places(mb | core, *zb),)
        mass = add_masses(documents, mass, (other,), places, devices)
    return score(2, 16, True, documents[-1], mass)


def whole_body(hidden, segment, counts, w_proj, seeds):
    own = lax.all_gather(unit_rows(seeds), "shard", axis=1, tiled=True)
    every = lax.all_gather(own, "loop", axis=0, tiled=True)
    tokens = every.shape[1]
    every = every.reshape(-1, every.shape[-1])
    pieces = every.shape[0] // PIECE
    documents = regroup_documents(hidden, counts, w_proj)
    mass = None
    for first in range(0, pieces, 4):
        places = (tuple(range(first, first + 4)),)
        chunk = every[first * PIECE : (first + 4) * PIECE]
        mass = add_masses(documents, mass, (chunk,), places, pieces)
    return score(1, tokens, False, documents[-1], mass)


def solution(mesh):
    in_specs = (
        P(("shard", "loop"), None),
        P(("shard", "loop")),
        P(("shard", "loop")),
        P(),
        P("loop", "shard", None),
    )
    out_specs = P(("shard", "loop"), None)
    paired = mesh.shape["shard"] == 2 and mesh.shape["loop"] == 16
    body = pair_body if paired else whole_body
    return jax.shard_map(body, mesh=mesh, in_specs=in_specs, out_specs=out_specs, check_vma=False)
```

```python
import functools

import jax
import jax.numpy as jnp
from jax import lax
from jax.experimental import pallas as pl
from jax.experimental.pallas import tpu as pltpu
from jax.sharding import PartitionSpec as P

BETA = 16.0
EPS = 1e-06
LOG2E = 1.4426950408889634
GROUP = 16
HALF = GROUP // 2
PIECE = 256
LANES = 128
ANY = pl.BlockSpec(memory_space=pl.ANY)
VMEM = pl.BlockSpec(memory_space=pltpu.VMEM)


def unit_rows(values):
    values = values.astype(jnp.float32)
    return (values * lax.rsqrt(jnp.sum(values * values, axis=-1, keepdims=True) + EPS)).astype(
        jnp.bfloat16
    )


def params(mib):
    return pltpu.CompilerParams(vmem_limit_bytes=mib * 2**20)


def cost(micros):
    return pl.CostEstimate(flops=int(micros * 1e6), bytes_accessed=0, transcendentals=0)


def layout_kernel(counts_any, inside, keep, last, lengths, counts, sem):
    docs, groups = last.shape[0], keep.shape[0]
    fetch = pltpu.make_async_copy(counts_any, counts, sem)
    fetch.start()
    fetch.wait()
    group = lax.broadcasted_iota(jnp.int32, keep.shape, 0)
    document = lax.broadcasted_iota(jnp.int32, last.shape, 0)
    place = lax.broadcasted_iota(jnp.int32, (GROUP, LANES), 0)
    keeps = jnp.ones(keep.shape, jnp.float32)
    lasts = jnp.zeros(last.shape, jnp.int32)
    sizes = jnp.zeros(last.shape, jnp.float32)
    first = jnp.int32(0)
    for d in range(docs):
        count = counts[d]
        full = count // GROUP
        inside[d * GROUP : (d + 1) * GROUP, :] = (place < count - full * GROUP).astype(jnp.float32)
        keeps = jnp.where(group == jnp.where(full > 0, first, groups), 0.0, keeps)
        lasts = jnp.where(document == d, jnp.where(full > 0, first + full - 1, groups), lasts)
        sizes = jnp.where(document == d, count.astype(jnp.float32), sizes)
        first = first + full
    keep[...] = keeps
    last[...] = lasts
    lengths[...] = sizes


def document_layout(counts, rows):
    docs, groups = counts.shape[0], rows // GROUP
    return pl.pallas_call(
        layout_kernel,
        out_shape=(
            jax.ShapeDtypeStruct((docs * GROUP, LANES), jnp.float32),
            jax.ShapeDtypeStruct((groups, LANES), jnp.float32),
            jax.ShapeDtypeStruct((docs, LANES), jnp.int32),
            jax.ShapeDtypeStruct((docs, LANES), jnp.float32),
        ),
        in_specs=[ANY],
        out_specs=(VMEM,) * 4,
        scratch_shapes=[pltpu.SMEM((docs,), jnp.int32), pltpu.SemaphoreType.DMA],
        compiler_params=params(4),
        cost_estimate=cost(20000),
        name="layout",
    )(pltpu.with_memory_space_constraint(counts, pltpu.HBM))


def docs_kernel(counts_any, hidden, w_proj, rows_out, vectors, counts, sem):
    docs = counts.shape[0]
    rows = hidden.shape[0]
    tail = docs * GROUP
    fetch = pltpu.make_async_copy(counts_any, counts, sem)
    fetch.start()
    step = 384 if rows % 384 == 0 else rows
    for lo in range(0, rows, step):
        block = slice(lo, lo + step)
        projected = jnp.dot(hidden[block, :], w_proj[...], preferred_element_type=jnp.float32)
        vectors[block, :] = unit_rows(projected).astype(jnp.float32)
    vectors[rows:, :] = jnp.zeros_like(vectors[rows:, :])
    rows_out[tail:, :] = jnp.zeros_like(rows_out[tail:, :])
    fetch.wait()
    start = jnp.int32(0)
    first = jnp.int32(0)
    for d in range(docs):
        count = counts[d]
        full = count // GROUP

        def move(k, carry, start=start, first=first):
            block = vectors[pl.ds(start + k * GROUP, GROUP), :]
            at = pl.multiple_of(tail + (first + k) * GROUP, GROUP)
            rows_out[pl.ds(at, GROUP), :] = block.astype(jnp.bfloat16)
            return carry

        lax.fori_loop(0, full, move, 0)
        block = vectors[pl.ds(start + full * GROUP, GROUP), :]
        rows_out[d * GROUP : (d + 1) * GROUP, :] = block.astype(jnp.bfloat16)
        start = start + count
        first = first + full


def regroup_documents(hidden, counts, w_proj):
    rows, docs = hidden.shape[0], counts.shape[0]
    width = w_proj.shape[1]
    return pl.pallas_call(
        docs_kernel,
        out_shape=jax.ShapeDtypeStruct((docs * GROUP + rows, width), jnp.bfloat16),
        in_specs=[ANY, VMEM, VMEM],
        out_specs=VMEM,
        scratch_shapes=[
            pltpu.VMEM((rows + GROUP, width), jnp.float32),
            pltpu.SMEM((docs,), jnp.int32),
            pltpu.SemaphoreType.DMA,
        ],
        compiler_params=params(16),
        cost_estimate=cost(2.5),
        name="documents",
    )(pltpu.with_memory_space_constraint(counts, pltpu.HBM), hidden, w_proj)


def unit_kernel(*refs):
    *pieces, out = refs
    for i, piece in enumerate(pieces):
        values = piece[...].reshape(PIECE, piece.shape[-1])
        out[i * PIECE : (i + 1) * PIECE, :] = unit_rows(values)


def unit_pieces(*pieces):
    return pl.pallas_call(
        unit_kernel,
        out_shape=jax.ShapeDtypeStruct((len(pieces) * PIECE, pieces[0].shape[-1]), jnp.bfloat16),
        in_specs=[VMEM] * len(pieces),
        out_specs=VMEM,
        compiler_params=params(8),
        cost_estimate=cost(0.2),
        name="unit_pieces",
    )(*pieces)


def mass_kernel(places, rows, inside, keep, last, *refs):
    *chunks, mass, sums, tail_sums = refs
    chunks = chunks[-len(places) :]
    docs = last.shape[0]
    groups = keep.shape[0]
    tail = docs * GROUP

    def weights(block, tokens):
        sims = lax.dot_general(
            block, tokens, (((1,), (1,)), ((), ())), preferred_element_type=jnp.float32
        )
        return jnp.exp2(sims * (BETA * LOG2E))

    def wide(row, width):
        return jnp.concatenate([row] * (width // LANES), axis=1)

    step = 24 if groups % 24 == 0 else groups
    ends = last[...]
    for c, chunk in enumerate(chunks):
        tokens = chunk[...]
        width = tokens.shape[0]
        block = weights(rows[:tail, :], tokens)
        for d in range(docs):
            lo = d * GROUP
            mid, hi = lo + HALF, lo + GROUP
            tail_sums[c, d] = block[lo:mid] * wide(inside[lo:mid, :], width) + block[
                mid:hi
            ] * wide(inside[mid:hi, :], width)
        total = jnp.zeros((HALF, width), jnp.float32)
        sums[c, groups] = total
        for base in range(0, groups, step):
            block = weights(rows[tail + base * GROUP : tail + (base + step) * GROUP, :], tokens)
            for j in range(step):
                lo = j * GROUP
                mid, hi = lo + HALF, lo + GROUP
                row = jnp.broadcast_to(keep[base + j : base + j + 1, :], (HALF, LANES))
                total = total * wide(row, width) + (block[lo:mid] + block[mid:hi])
                sums[c, base + j] = total
    odd = lax.axis_index("loop") % 2
    for c, place in enumerate(places):
        at = [even if even == other else jnp.where(odd == 0, even, other) for even, other in place]
        for d in range(docs):
            total = jnp.sum(sums[c, ends[d, 0]] + tail_sums[c, d], axis=0, keepdims=True)
            for i, piece in enumerate(at):
                mass[piece, d : d + 1, :] = total[:, i * PIECE : (i + 1) * PIECE]


def add_masses(documents, mass, chunks, places, pieces):
    rows, inside, keep, last, _ = documents
    docs, groups = last.shape[0], keep.shape[0]
    count, width = len(chunks), chunks[0].shape[0]
    before = () if mass is None else (mass,)
    return pl.pallas_call(
        functools.partial(mass_kernel, places),
        out_shape=jax.ShapeDtypeStruct((pieces, docs, PIECE), jnp.float32),
        in_specs=[VMEM] * (4 + len(before) + count),
        out_specs=VMEM,
        input_output_aliases={4: 0} if before else {},
        scratch_shapes=[
            pltpu.VMEM((count, groups + 1, HALF, width), jnp.float32),
            pltpu.VMEM((count, docs, HALF, width), jnp.float32),
        ],
        compiler_params=params(28),
        cost_estimate=cost(20000),
        name="masses",
    )(rows, inside, keep, last, *before, *chunks)


def score_kernel(parts, tokens, relative, lengths, mass, scores):
    pieces, docs, _ = mass.shape
    groups = pieces // parts
    queries = PIECE // tokens
    per_tile = LANES // queries
    tiles = groups // per_tile
    own = lax.axis_index("loop") if relative else 0
    sizes = jnp.concatenate([lengths[...]] * (PIECE // LANES), axis=1)
    place = lax.broadcasted_iota(jnp.int32, (PIECE, LANES), 0) // tokens
    column = lax.broadcasted_iota(jnp.int32, (PIECE, LANES), 1)
    total = jnp.zeros((tiles * docs, LANES), jnp.float32)
    for i in range(per_tile):
        logs = []
        for tile in range(tiles):
            at = ((tile * per_tile + i) ^ own) * parts
            logs.append(sum(jnp.log(mass[at + part] / sizes) for part in range(parts)))
        rest = jnp.concatenate(logs, axis=0)
        pick = (column == place + i * queries).astype(jnp.bfloat16)
        for _ in range(3):
            head = rest.astype(jnp.bfloat16)
            total = total + jnp.dot(head, pick, preferred_element_type=jnp.float32)
            rest = rest - head.astype(jnp.float32)
    total = total * (1.0 / (tokens * parts))
    for tile in range(tiles):
        scores[:, tile * LANES : (tile + 1) * LANES] = total[tile * docs : (tile + 1) * docs]


def score(parts, tokens, relative, lengths, mass):
    pieces, docs, _ = mass.shape
    queries = pieces // parts * (PIECE // tokens)
    return pl.pallas_call(
        functools.partial(score_kernel, parts, tokens, relative),
        out_shape=jax.ShapeDtypeStruct((docs, queries), jnp.float32),
        in_specs=[VMEM, VMEM],
        out_specs=VMEM,
        compiler_params=params(8),
        cost_estimate=cost(1),
        name="scores",
    )(lengths, mass)


def swap(values, even, odd=None):
    odd = even if odd is None else odd
    pairs = [(i, i ^ (even if i % 2 == 0 else odd)) for i in range(32)]
    return lax.ppermute(values, ("shard", "loop"), pairs)


def pair_body(hidden, segment, counts, w_proj, seeds):
    devices = 32
    core, x, z, far, y = 1, 2, 4, 8, 16
    after = lax.optimization_barrier
    raw_far = swap(seeds, far)
    raw_z = swap(seeds, z)
    layout = document_layout(counts, hidden.shape[0])
    raw_far, layout = after((raw_far, layout))
    raw_both = swap(raw_far, z)
    near = unit_pieces(seeds, raw_z)
    first_near = swap(near, x, y)
    away = unit_pieces(raw_far, raw_both)
    first_away = swap(away, x, y)
    own = jnp.concatenate([near, away], axis=0)
    own_core = swap(own, core)
    hidden, away = after((hidden, away))
    rows = regroup_documents(hidden, counts, w_proj)
    documents = (rows, *layout)

    def add(mass, chunk, masks, through_core):
        if through_core:
            masks = (masks[1] ^ core, masks[0] ^ core)
        place = tuple(
            tuple(((mask & 15) ^ bits) * 2 + (mask >> 4) for mask in masks)
            for bits in (0, z, far, z | far)
        )
        return add_masses(documents, mass, (chunk,), (place,), devices)

    mass = add(None, own, (0, 0), False)
    first_near, first_away, own, mass = after((first_near, first_away, own, mass))
    first = jnp.concatenate([first_near, first_away], axis=0)
    third = swap(first, y, x)
    second = swap(own, y, x)
    first_core = swap(first, core)
    mass = add(mass, own_core, (0, 0), True)
    mass = add(mass, first, (x, y), False)
    mass = add(mass, first_core, (x, y), True)
    third, mass = after((third, mass))
    third_core = swap(third, core)
    mass = add(mass, third, (x | y, x | y), False)
    mass = add(mass, third_core, (x | y, x | y), True)
    second, mass = after((second, mass))
    second_core = swap(second, core)
    mass = add(mass, second, (y, x), False)
    mass = add(mass, second_core, (y, x), True)
    return score(2, 16, True, documents[-1], mass)


def whole_body(hidden, segment, counts, w_proj, seeds):
    own = lax.all_gather(unit_rows(seeds), "shard", axis=1, tiled=True)
    every = lax.all_gather(own, "loop", axis=0, tiled=True)
    tokens = every.shape[1]
    every = every.reshape(-1, every.shape[-1])
    pieces = every.shape[0] // PIECE
    layout = document_layout(counts, hidden.shape[0])
    documents = (regroup_documents(hidden, counts, w_proj), *layout)
    mass = None
    for first in range(0, pieces, 4):
        places = (tuple((piece, piece) for piece in range(first, first + 4)),)
        chunk = every[first * PIECE : (first + 4) * PIECE]
        mass = add_masses(documents, mass, (chunk,), places, pieces)
    return score(1, tokens, False, documents[-1], mass)


def solution(mesh):
    in_specs = (
        P(("shard", "loop"), None),
        P(("shard", "loop")),
        P(("shard", "loop")),
        P(),
        P("loop", "shard", None),
    )
    out_specs = P(("shard", "loop"), None)
    paired = mesh.shape["shard"] == 2 and mesh.shape["loop"] == 16
    body = pair_body if paired else whole_body
    return jax.shard_map(body, mesh=mesh, in_specs=in_specs, out_specs=out_specs, check_vma=False)
```

```python
import functools

import jax
import jax.numpy as jnp
from jax import lax
from jax.experimental import pallas as pl
from jax.experimental.pallas import tpu as pltpu
from jax.sharding import PartitionSpec as P

BETA = 16.0
EPS = 1e-06
LOG2E = 1.4426950408889634
GROUP = 16
HALF = GROUP // 2
PIECE = 256
LANES = 128
ANY = pl.BlockSpec(memory_space=pl.ANY)
VMEM = pl.BlockSpec(memory_space=pltpu.VMEM)


def unit_rows(values):
    values = values.astype(jnp.float32)
    return (values * lax.rsqrt(jnp.sum(values * values, axis=-1, keepdims=True) + EPS)).astype(
        jnp.bfloat16
    )


def params(mib):
    return pltpu.CompilerParams(vmem_limit_bytes=mib * 2**20)


def cost(micros):
    return pl.CostEstimate(flops=int(micros * 1e6), bytes_accessed=0, transcendentals=0)


def layout_kernel(counts_any, inside, keep, last, lengths, counts, sem):
    docs, groups = last.shape[0], keep.shape[0]
    fetch = pltpu.make_async_copy(counts_any, counts, sem)
    fetch.start()
    fetch.wait()
    group = lax.broadcasted_iota(jnp.int32, keep.shape, 0)
    document = lax.broadcasted_iota(jnp.int32, last.shape, 0)
    place = lax.broadcasted_iota(jnp.int32, (GROUP, LANES), 0)
    keeps = jnp.ones(keep.shape, jnp.float32)
    lasts = jnp.zeros(last.shape, jnp.int32)
    sizes = jnp.zeros(last.shape, jnp.float32)
    first = jnp.int32(0)
    for d in range(docs):
        count = counts[d]
        full = count // GROUP
        inside[d * GROUP : (d + 1) * GROUP, :] = (place < count - full * GROUP).astype(jnp.float32)
        keeps = jnp.where(group == jnp.where(full > 0, first, groups), 0.0, keeps)
        lasts = jnp.where(document == d, jnp.where(full > 0, first + full - 1, groups), lasts)
        sizes = jnp.where(document == d, count.astype(jnp.float32), sizes)
        first = first + full
    keep[...] = keeps
    last[...] = lasts
    lengths[...] = sizes


def document_layout(counts, rows):
    docs, groups = counts.shape[0], rows // GROUP
    return pl.pallas_call(
        layout_kernel,
        out_shape=(
            jax.ShapeDtypeStruct((docs * GROUP, LANES), jnp.float32),
            jax.ShapeDtypeStruct((groups, LANES), jnp.float32),
            jax.ShapeDtypeStruct((docs, LANES), jnp.int32),
            jax.ShapeDtypeStruct((docs, LANES), jnp.float32),
        ),
        in_specs=[ANY],
        out_specs=(VMEM,) * 4,
        scratch_shapes=[pltpu.SMEM((docs,), jnp.int32), pltpu.SemaphoreType.DMA],
        compiler_params=params(4),
        cost_estimate=cost(20000),
        name="layout",
    )(pltpu.with_memory_space_constraint(counts, pltpu.HBM))


def docs_kernel(counts_any, hidden, w_proj, rows_out, vectors, counts, sem):
    docs = counts.shape[0]
    rows = hidden.shape[0]
    tail = docs * GROUP
    fetch = pltpu.make_async_copy(counts_any, counts, sem)
    fetch.start()
    step = 384 if rows % 384 == 0 else rows
    for lo in range(0, rows, step):
        block = slice(lo, lo + step)
        projected = jnp.dot(hidden[block, :], w_proj[...], preferred_element_type=jnp.float32)
        vectors[block, :] = unit_rows(projected).astype(jnp.float32)
    vectors[rows:, :] = jnp.zeros_like(vectors[rows:, :])
    rows_out[tail:, :] = jnp.zeros_like(rows_out[tail:, :])
    fetch.wait()
    start = jnp.int32(0)
    first = jnp.int32(0)
    for d in range(docs):
        count = counts[d]
        full = count // GROUP

        def move(k, carry, start=start, first=first):
            block = vectors[pl.ds(start + k * GROUP, GROUP), :]
            at = pl.multiple_of(tail + (first + k) * GROUP, GROUP)
            rows_out[pl.ds(at, GROUP), :] = block.astype(jnp.bfloat16)
            return carry

        lax.fori_loop(0, full, move, 0)
        block = vectors[pl.ds(start + full * GROUP, GROUP), :]
        rows_out[d * GROUP : (d + 1) * GROUP, :] = block.astype(jnp.bfloat16)
        start = start + count
        first = first + full


def regroup_documents(hidden, counts, w_proj):
    rows, docs = hidden.shape[0], counts.shape[0]
    width = w_proj.shape[1]
    return pl.pallas_call(
        docs_kernel,
        out_shape=jax.ShapeDtypeStruct((docs * GROUP + rows, width), jnp.bfloat16),
        in_specs=[ANY, VMEM, VMEM],
        out_specs=VMEM,
        scratch_shapes=[
            pltpu.VMEM((rows + GROUP, width), jnp.float32),
            pltpu.SMEM((docs,), jnp.int32),
            pltpu.SemaphoreType.DMA,
        ],
        compiler_params=params(16),
        cost_estimate=cost(2.5),
        name="documents",
    )(pltpu.with_memory_space_constraint(counts, pltpu.HBM), hidden, w_proj)


def unit_kernel(*refs):
    *pieces, out = refs
    for i, piece in enumerate(pieces):
        values = piece[...].reshape(PIECE, piece.shape[-1])
        out[i * PIECE : (i + 1) * PIECE, :] = unit_rows(values)


def unit_pieces(*pieces):
    return pl.pallas_call(
        unit_kernel,
        out_shape=jax.ShapeDtypeStruct((len(pieces) * PIECE, pieces[0].shape[-1]), jnp.bfloat16),
        in_specs=[VMEM] * len(pieces),
        out_specs=VMEM,
        compiler_params=params(8),
        cost_estimate=cost(0.2),
        name="unit_pieces",
    )(*pieces)


def mass_kernel(places, rows, inside, keep, last, *refs):
    *chunks, mass, sums, tail_sums = refs
    chunks = chunks[-len(places) :]
    docs = last.shape[0]
    groups = keep.shape[0]
    tail = docs * GROUP

    def weights(block, tokens):
        sims = lax.dot_general(
            block, tokens, (((1,), (1,)), ((), ())), preferred_element_type=jnp.float32
        )
        return jnp.exp2(sims * (BETA * LOG2E))

    def wide(row, width):
        return jnp.concatenate([row] * (width // LANES), axis=1)

    step = 24 if groups % 24 == 0 else groups
    ends = last[...]
    for c, chunk in enumerate(chunks):
        tokens = chunk[...]
        width = tokens.shape[0]
        block = weights(rows[:tail, :], tokens)
        for d in range(docs):
            lo = d * GROUP
            mid, hi = lo + HALF, lo + GROUP
            tail_sums[c, d] = block[lo:mid] * wide(inside[lo:mid, :], width) + block[
                mid:hi
            ] * wide(inside[mid:hi, :], width)
        total = jnp.zeros((HALF, width), jnp.float32)
        sums[c, groups] = total
        for base in range(0, groups, step):
            block = weights(rows[tail + base * GROUP : tail + (base + step) * GROUP, :], tokens)
            for j in range(step):
                lo = j * GROUP
                mid, hi = lo + HALF, lo + GROUP
                row = jnp.broadcast_to(keep[base + j : base + j + 1, :], (HALF, LANES))
                total = total * wide(row, width) + (block[lo:mid] + block[mid:hi])
                sums[c, base + j] = total
    odd = lax.axis_index("loop") % 2
    for c, place in enumerate(places):
        at = [even if even == other else jnp.where(odd == 0, even, other) for even, other in place]
        for d in range(docs):
            total = jnp.sum(sums[c, ends[d, 0]] + tail_sums[c, d], axis=0, keepdims=True)
            for i, piece in enumerate(at):
                mass[piece, d : d + 1, :] = total[:, i * PIECE : (i + 1) * PIECE]


def add_masses(documents, mass, chunks, places, pieces):
    rows, inside, keep, last, _ = documents
    docs, groups = last.shape[0], keep.shape[0]
    count, width = len(chunks), chunks[0].shape[0]
    before = () if mass is None else (mass,)
    return pl.pallas_call(
        functools.partial(mass_kernel, places),
        out_shape=jax.ShapeDtypeStruct((pieces, docs, PIECE), jnp.float32),
        in_specs=[VMEM] * (4 + len(before) + count),
        out_specs=VMEM,
        input_output_aliases={4: 0} if before else {},
        scratch_shapes=[
            pltpu.VMEM((count, groups + 1, HALF, width), jnp.float32),
            pltpu.VMEM((count, docs, HALF, width), jnp.float32),
        ],
        compiler_params=params(28),
        cost_estimate=cost(20000),
        name="masses",
    )(rows, inside, keep, last, *before, *chunks)


def score_kernel(parts, tokens, relative, lengths, mass, scores):
    pieces, docs, _ = mass.shape
    groups = pieces // parts
    queries = PIECE // tokens
    per_tile = LANES // queries
    tiles = groups // per_tile
    own = lax.axis_index("loop") if relative else 0
    sizes = jnp.concatenate([lengths[...]] * (PIECE // LANES), axis=1)
    place = lax.broadcasted_iota(jnp.int32, (PIECE, LANES), 0) // tokens
    column = lax.broadcasted_iota(jnp.int32, (PIECE, LANES), 1)
    total = jnp.zeros((tiles * docs, LANES), jnp.float32)
    for i in range(per_tile):
        logs = []
        for tile in range(tiles):
            at = ((tile * per_tile + i) ^ own) * parts
            logs.append(sum(jnp.log(mass[at + part] / sizes) for part in range(parts)))
        rest = jnp.concatenate(logs, axis=0)
        pick = (column == place + i * queries).astype(jnp.bfloat16)
        for _ in range(3):
            head = rest.astype(jnp.bfloat16)
            total = total + jnp.dot(head, pick, preferred_element_type=jnp.float32)
            rest = rest - head.astype(jnp.float32)
    total = total * (1.0 / (tokens * parts))
    for tile in range(tiles):
        scores[:, tile * LANES : (tile + 1) * LANES] = total[tile * docs : (tile + 1) * docs]


def score(parts, tokens, relative, lengths, mass):
    pieces, docs, _ = mass.shape
    queries = pieces // parts * (PIECE // tokens)
    return pl.pallas_call(
        functools.partial(score_kernel, parts, tokens, relative),
        out_shape=jax.ShapeDtypeStruct((docs, queries), jnp.float32),
        in_specs=[VMEM, VMEM],
        out_specs=VMEM,
        compiler_params=params(8),
        cost_estimate=cost(1),
        name="scores",
    )(lengths, mass)


def swap(values, even, odd=None):
    odd = even if odd is None else odd
    pairs = [(i, i ^ (even if i % 2 == 0 else odd)) for i in range(32)]
    return lax.ppermute(values, ("shard", "loop"), pairs)


def pair_body(hidden, segment, counts, w_proj, seeds):
    devices = 32
    core, x, z, far, y = 1, 2, 4, 8, 16
    after = lax.optimization_barrier
    raw_far = swap(seeds, far, x)
    raw_z = swap(seeds, z, y)
    layout = document_layout(counts, hidden.shape[0])
    raw_far, layout = after((raw_far, layout))
    raw_both = swap(raw_far, z, y)
    near = unit_pieces(seeds, raw_z)
    first_near = swap(near, x, far)
    away = unit_pieces(raw_far, raw_both)
    first_away = swap(away, x, far)
    own = jnp.concatenate([near, away], axis=0)
    own_core = swap(own, core)
    hidden, away = after((hidden, away))
    rows = regroup_documents(hidden, counts, w_proj)
    documents = (rows, *layout)

    def add(mass, chunk, masks, through_core):
        lanes = [
            [mask ^ bits for bits in (0, one, two, one | two)]
            for mask, one, two in ((masks[0], z, far), (masks[1], y, x))
        ]
        if through_core:
            lanes = [[mask ^ core for mask in lane] for lane in lanes[::-1]]
        place = tuple(
            tuple((mask & 15) * 2 + (mask >> 4) for mask in pair) for pair in zip(*lanes)
        )
        return add_masses(documents, mass, (chunk,), (place,), devices)

    mass = add(None, own, (0, 0), False)
    first_near, first_away, own, mass = after((first_near, first_away, own, mass))
    first = jnp.concatenate([first_near, first_away], axis=0)
    third = swap(first, y, z)
    second = swap(own, y, z)
    first_core = swap(first, core)
    mass = add(mass, own_core, (0, 0), True)
    mass = add(mass, first, (x, far), False)
    mass = add(mass, first_core, (x, far), True)
    third, mass = after((third, mass))
    third_core = swap(third, core)
    mass = add(mass, third, (x | y, z | far), False)
    mass = add(mass, third_core, (x | y, z | far), True)
    second, mass = after((second, mass))
    second_core = swap(second, core)
    mass = add(mass, second, (y, z), False)
    mass = add(mass, second_core, (y, z), True)
    return score(2, 16, True, documents[-1], mass)


def whole_body(hidden, segment, counts, w_proj, seeds):
    own = lax.all_gather(unit_rows(seeds), "shard", axis=1, tiled=True)
    every = lax.all_gather(own, "loop", axis=0, tiled=True)
    tokens = every.shape[1]
    every = every.reshape(-1, every.shape[-1])
    pieces = every.shape[0] // PIECE
    layout = document_layout(counts, hidden.shape[0])
    documents = (regroup_documents(hidden, counts, w_proj), *layout)
    mass = None
    for first in range(0, pieces, 4):
        places = (tuple((piece, piece) for piece in range(first, first + 4)),)
        chunk = every[first * PIECE : (first + 4) * PIECE]
        mass = add_masses(documents, mass, (chunk,), places, pieces)
    return score(1, tokens, False, documents[-1], mass)


def solution(mesh):
    in_specs = (
        P(("shard", "loop"), None),
        P(("shard", "loop")),
        P(("shard", "loop")),
        P(),
        P("loop", "shard", None),
    )
    out_specs = P(("shard", "loop"), None)
    paired = mesh.shape["shard"] == 2 and mesh.shape["loop"] == 16
    body = pair_body if paired else whole_body
    return jax.shard_map(body, mesh=mesh, in_specs=in_specs, out_specs=out_specs, check_vma=False)
```

```python
import functools

import jax
import jax.numpy as jnp
from jax import lax
from jax.experimental import pallas as pl
from jax.experimental.pallas import tpu as pltpu
from jax.sharding import PartitionSpec as P

BETA = 16.0
EPS = 1e-06
LOG2E = 1.4426950408889634
GROUP = 16
HALF = GROUP // 2
PIECE = 256
LANES = 128
STEP = 24
SIZES = (84, 100)
BLOCK = 64
ANY = pl.BlockSpec(memory_space=pl.ANY)
VMEM = pl.BlockSpec(memory_space=pltpu.VMEM)
SMEM = pl.BlockSpec(memory_space=pltpu.SMEM)


def unit_rows(values):
    values = values.astype(jnp.float32)
    return (values * lax.rsqrt(jnp.sum(values * values, axis=-1, keepdims=True) + EPS)).astype(
        jnp.bfloat16
    )


def params(mib):
    return pltpu.CompilerParams(vmem_limit_bytes=mib * 2**20)


def cost(micros):
    return pl.CostEstimate(flops=int(micros * 1e6), bytes_accessed=0, transcendentals=0)


def layout_kernel(counts_any, inside, keep, last, lengths, counts, sem):
    docs, groups = counts.shape[0], keep.shape[0]
    fetch = pltpu.make_async_copy(counts_any, counts, sem)
    fetch.start()
    fetch.wait()
    group = lax.broadcasted_iota(jnp.int32, keep.shape, 0)
    document = lax.broadcasted_iota(jnp.int32, lengths.shape, 0)
    place = lax.broadcasted_iota(jnp.int32, (GROUP, LANES), 0)
    keeps = jnp.ones(keep.shape, jnp.float32)
    sizes = jnp.zeros(lengths.shape, jnp.float32)
    first = jnp.int32(0)
    for d in range(docs):
        count = counts[d]
        full = count // GROUP
        inside[d * GROUP : (d + 1) * GROUP, :] = (place < count - full * GROUP).astype(jnp.float32)
        keeps = jnp.where(group == jnp.where(full > 0, first, groups), 0.0, keeps)
        sizes = jnp.where(document == d, count.astype(jnp.float32), sizes)
        first = first + full
    keep[...] = keeps
    first = jnp.int32(0)
    for d in range(docs):
        full = counts[d] // GROUP
        last[d] = jnp.where(full > 0, first + full - 1, groups)
        first = first + full
    last[docs] = first
    lengths[...] = sizes


def document_layout(counts, rows):
    docs, groups = counts.shape[0], rows // GROUP
    return pl.pallas_call(
        layout_kernel,
        out_shape=(
            jax.ShapeDtypeStruct((docs * GROUP, LANES), jnp.float32),
            jax.ShapeDtypeStruct((groups, LANES), jnp.float32),
            pltpu.SMEM((docs + 1,), jnp.int32),
            jax.ShapeDtypeStruct((docs, LANES), jnp.float32),
        ),
        in_specs=[ANY],
        out_specs=(VMEM, VMEM, SMEM, VMEM),
        scratch_shapes=[pltpu.SMEM((docs,), jnp.int32), pltpu.SemaphoreType.DMA],
        compiler_params=params(4),
        cost_estimate=cost(20000),
        name="layout",
    )(pltpu.with_memory_space_constraint(counts, pltpu.HBM))


def docs_kernel(counts_any, hidden, w_proj, rows_out, vectors, counts, sem):
    docs = counts.shape[0]
    rows = hidden.shape[0]
    tail = docs * GROUP
    fetch = pltpu.make_async_copy(counts_any, counts, sem)
    fetch.start()
    step = 384 if rows % 384 == 0 else rows
    for lo in range(0, rows, step):
        block = slice(lo, lo + step)
        projected = jnp.dot(hidden[block, :], w_proj[...], preferred_element_type=jnp.float32)
        vectors[block, :] = unit_rows(projected).astype(jnp.float32)
    vectors[rows:, :] = jnp.zeros_like(vectors[rows:, :])
    rows_out[tail:, :] = jnp.zeros_like(rows_out[tail:, :])
    fetch.wait()
    start = jnp.int32(0)
    first = jnp.int32(0)
    for d in range(docs):
        count = counts[d]
        full = count // GROUP

        def move(k, carry, start=start, first=first):
            block = vectors[pl.ds(start + k * BLOCK, BLOCK), :]
            at = pl.multiple_of(tail + first * GROUP + k * BLOCK, GROUP)
            rows_out[pl.ds(at, BLOCK), :] = block.astype(jnp.bfloat16)
            return carry

        lax.fori_loop(0, (full * GROUP + BLOCK - 1) // BLOCK, move, 0)
        block = vectors[pl.ds(start + full * GROUP, GROUP), :]
        rows_out[d * GROUP : (d + 1) * GROUP, :] = block.astype(jnp.bfloat16)
        start = start + count
        first = first + full


def regroup_documents(hidden, counts, w_proj):
    rows, docs = hidden.shape[0], counts.shape[0]
    width = w_proj.shape[1]
    return pl.pallas_call(
        docs_kernel,
        out_shape=jax.ShapeDtypeStruct((docs * GROUP + rows + BLOCK, width), jnp.bfloat16),
        in_specs=[ANY, VMEM, VMEM],
        out_specs=VMEM,
        scratch_shapes=[
            pltpu.VMEM((rows + BLOCK, width), jnp.float32),
            pltpu.SMEM((docs,), jnp.int32),
            pltpu.SemaphoreType.DMA,
        ],
        compiler_params=params(16),
        cost_estimate=cost(2.5),
        name="documents",
    )(pltpu.with_memory_space_constraint(counts, pltpu.HBM), hidden, w_proj)


def unit_kernel(*refs):
    *pieces, out = refs
    for i, piece in enumerate(pieces):
        values = piece[...].reshape(PIECE, piece.shape[-1])
        out[i * PIECE : (i + 1) * PIECE, :] = unit_rows(values)


def unit_pieces(*pieces):
    return pl.pallas_call(
        unit_kernel,
        out_shape=jax.ShapeDtypeStruct((len(pieces) * PIECE, pieces[0].shape[-1]), jnp.bfloat16),
        in_specs=[VMEM] * len(pieces),
        out_specs=VMEM,
        compiler_params=params(8),
        cost_estimate=cost(0.2),
        name="unit_pieces",
    )(*pieces)


def mass_kernel(places, rows, inside, keep, last, *refs):
    *chunks, mass, sums, tail_sums = refs
    chunks = chunks[-len(places) :]
    docs = last.shape[0] - 1
    groups = keep.shape[0]
    tail = docs * GROUP

    def weights(block, tokens):
        sims = lax.dot_general(
            block, tokens, (((1,), (1,)), ((), ())), preferred_element_type=jnp.float32
        )
        return jnp.exp2(sims * (BETA * LOG2E))

    def wide(row, width):
        return jnp.concatenate([row] * (width // LANES), axis=1)

    used = last[docs]
    for c, chunk in enumerate(chunks):
        width = chunk.shape[0]
        sums[c, groups] = jnp.zeros((HALF, width), jnp.float32)

    def run(size):
        for c, chunk in enumerate(chunks):
            tokens = chunk[...]
            width = tokens.shape[0]
            block = weights(rows[:tail, :], tokens)
            for d in range(docs):
                lo = d * GROUP
                mid, hi = lo + HALF, lo + GROUP
                tail_sums[c, d] = block[lo:mid] * wide(inside[lo:mid, :], width) + block[
                    mid:hi
                ] * wide(inside[mid:hi, :], width)
            total = jnp.zeros((HALF, width), jnp.float32)
            for base in range(0, size, STEP):
                step = min(STEP, size - base)
                block = weights(rows[tail + base * GROUP : tail + (base + step) * GROUP, :], tokens)
                for j in range(step):
                    lo = j * GROUP
                    mid, hi = lo + HALF, lo + GROUP
                    row = jnp.broadcast_to(keep[base + j : base + j + 1, :], (HALF, LANES))
                    total = total * wide(row, width) + (block[lo:mid] + block[mid:hi])
                    sums[c, base + j] = total

    sizes = [size for size in SIZES if size < groups] + [groups]
    for below, size in zip([-1] + sizes, sizes):
        pl.when((used > below) & (used <= size))(functools.partial(run, size))
    odd = lax.axis_index("loop") % 2
    for c, place in enumerate(places):
        at = [even if even == other else jnp.where(odd == 0, even, other) for even, other in place]
        for d in range(docs):
            total = jnp.sum(sums[c, last[d]] + tail_sums[c, d], axis=0, keepdims=True)
            for i, piece in enumerate(at):
                mass[piece, d : d + 1, :] = total[:, i * PIECE : (i + 1) * PIECE]


def add_masses(documents, mass, chunks, places, pieces):
    rows, inside, keep, last, _ = documents
    docs, groups = last.shape[0] - 1, keep.shape[0]
    last = pltpu.with_memory_space_constraint(last, pltpu.SMEM)
    count, width = len(chunks), chunks[0].shape[0]
    before = () if mass is None else (mass,)
    return pl.pallas_call(
        functools.partial(mass_kernel, places),
        out_shape=jax.ShapeDtypeStruct((pieces, docs, PIECE), jnp.float32),
        in_specs=[VMEM, VMEM, VMEM, SMEM] + [VMEM] * (len(before) + count),
        out_specs=VMEM,
        input_output_aliases={4: 0} if before else {},
        scratch_shapes=[
            pltpu.VMEM((count, groups + 1, HALF, width), jnp.float32),
            pltpu.VMEM((count, docs, HALF, width), jnp.float32),
        ],
        compiler_params=params(28),
        cost_estimate=cost(20000),
        name="masses",
    )(rows, inside, keep, last, *before, *chunks)


def score_kernel(parts, tokens, relative, lengths, mass, scores):
    pieces, docs, _ = mass.shape
    groups = pieces // parts
    queries = PIECE // tokens
    per_tile = LANES // queries
    tiles = groups // per_tile
    own = lax.axis_index("loop") if relative else 0
    sizes = jnp.concatenate([lengths[...]] * (PIECE // LANES), axis=1)
    place = lax.broadcasted_iota(jnp.int32, (PIECE, LANES), 0) // tokens
    column = lax.broadcasted_iota(jnp.int32, (PIECE, LANES), 1)
    total = jnp.zeros((tiles * docs, LANES), jnp.float32)
    for i in range(per_tile):
        logs = []
        for tile in range(tiles):
            at = ((tile * per_tile + i) ^ own) * parts
            logs.append(sum(jnp.log(mass[at + part] / sizes) for part in range(parts)))
        rest = jnp.concatenate(logs, axis=0)
        pick = (column == place + i * queries).astype(jnp.bfloat16)
        for _ in range(3):
            head = rest.astype(jnp.bfloat16)
            total = total + jnp.dot(head, pick, preferred_element_type=jnp.float32)
            rest = rest - head.astype(jnp.float32)
    total = total * (1.0 / (tokens * parts))
    for tile in range(tiles):
        scores[:, tile * LANES : (tile + 1) * LANES] = total[tile * docs : (tile + 1) * docs]


def score(parts, tokens, relative, lengths, mass):
    pieces, docs, _ = mass.shape
    queries = pieces // parts * (PIECE // tokens)
    return pl.pallas_call(
        functools.partial(score_kernel, parts, tokens, relative),
        out_shape=jax.ShapeDtypeStruct((docs, queries), jnp.float32),
        in_specs=[VMEM, VMEM],
        out_specs=VMEM,
        compiler_params=params(8),
        cost_estimate=cost(1),
        name="scores",
    )(lengths, mass)


def swap(values, even, odd=None):
    odd = even if odd is None else odd
    pairs = [(i, i ^ (even if i % 2 == 0 else odd)) for i in range(32)]
    return lax.ppermute(values, ("shard", "loop"), pairs)


def pair_body(hidden, segment, counts, w_proj, seeds):
    devices = 32
    core, x, z, far, y = 1, 2, 4, 8, 16
    after = lax.optimization_barrier
    raw_far = swap(seeds, far, x)
    raw_z = swap(seeds, z, y)
    layout = document_layout(counts, hidden.shape[0])
    raw_far, layout = after((raw_far, layout))
    raw_both = swap(raw_far, z, y)
    near = unit_pieces(seeds, raw_z)
    first_near = swap(near, x, far)
    away = unit_pieces(raw_far, raw_both)
    first_away = swap(away, x, far)
    own = jnp.concatenate([near, away], axis=0)
    own_core = swap(own, core)
    hidden, away = after((hidden, away))
    rows = regroup_documents(hidden, counts, w_proj)
    documents = (rows, *layout)

    def add(mass, chunk, masks, through_core):
        lanes = [
            [mask ^ bits for bits in (0, one, two, one | two)]
            for mask, one, two in ((masks[0], z, far), (masks[1], y, x))
        ]
        if through_core:
            lanes = [[mask ^ core for mask in lane] for lane in lanes[::-1]]
        place = tuple(
            tuple((mask & 15) * 2 + (mask >> 4) for mask in pair) for pair in zip(*lanes)
        )
        return add_masses(documents, mass, (chunk,), (place,), devices)

    mass = add(None, own, (0, 0), False)
    first_near, first_away, own, mass = after((first_near, first_away, own, mass))
    first = jnp.concatenate([first_near, first_away], axis=0)
    third = swap(first, y, z)
    second = swap(own, y, z)
    first_core = swap(first, core)
    mass = add(mass, own_core, (0, 0), True)
    mass = add(mass, first, (x, far), False)
    mass = add(mass, first_core, (x, far), True)
    third, mass = after((third, mass))
    third_core = swap(third, core)
    mass = add(mass, third, (x | y, z | far), False)
    mass = add(mass, third_core, (x | y, z | far), True)
    second, mass = after((second, mass))
    second_core = swap(second, core)
    mass = add(mass, second, (y, z), False)
    mass = add(mass, second_core, (y, z), True)
    return score(2, 16, True, documents[-1], mass)


def whole_body(hidden, segment, counts, w_proj, seeds):
    own = lax.all_gather(unit_rows(seeds), "shard", axis=1, tiled=True)
    every = lax.all_gather(own, "loop", axis=0, tiled=True)
    tokens = every.shape[1]
    every = every.reshape(-1, every.shape[-1])
    pieces = every.shape[0] // PIECE
    layout = document_layout(counts, hidden.shape[0])
    documents = (regroup_documents(hidden, counts, w_proj), *layout)
    mass = None
    for first in range(0, pieces, 4):
        places = (tuple((piece, piece) for piece in range(first, first + 4)),)
        chunk = every[first * PIECE : (first + 4) * PIECE]
        mass = add_masses(documents, mass, (chunk,), places, pieces)
    return score(1, tokens, False, documents[-1], mass)


def solution(mesh):
    in_specs = (
        P(("shard", "loop"), None),
        P(("shard", "loop")),
        P(("shard", "loop")),
        P(),
        P("loop", "shard", None),
    )
    out_specs = P(("shard", "loop"), None)
    paired = mesh.shape["shard"] == 2 and mesh.shape["loop"] == 16
    body = pair_body if paired else whole_body
    return jax.shard_map(body, mesh=mesh, in_specs=in_specs, out_specs=out_specs, check_vma=False)
```

```python
import functools

import jax
import jax.numpy as jnp
from jax import lax
from jax.experimental import pallas as pl
from jax.experimental.pallas import tpu as pltpu
from jax.sharding import PartitionSpec as P

BETA = 16.0
EPS = 1e-06
LOG2E = 1.4426950408889634
GROUP = 16
HALF = GROUP // 2
PIECE = 256
LANES = 128
STEP = 24
SIZES = (84, 100)
BLOCK = 64
ANY = pl.BlockSpec(memory_space=pl.ANY)
VMEM = pl.BlockSpec(memory_space=pltpu.VMEM)
SMEM = pl.BlockSpec(memory_space=pltpu.SMEM)


def unit_rows(values):
    values = values.astype(jnp.float32)
    return (values * lax.rsqrt(jnp.sum(values * values, axis=-1, keepdims=True) + EPS)).astype(
        jnp.bfloat16
    )


def params(mib):
    return pltpu.CompilerParams(vmem_limit_bytes=mib * 2**20)


def cost(micros):
    return pl.CostEstimate(flops=int(micros * 1e6), bytes_accessed=0, transcendentals=0)


def layout_kernel(counts_any, inside, keep, last, lengths, counts, sem):
    docs, groups = counts.shape[0], keep.shape[0]
    fetch = pltpu.make_async_copy(counts_any, counts, sem)
    fetch.start()
    fetch.wait()
    group = lax.broadcasted_iota(jnp.int32, keep.shape, 0)
    document = lax.broadcasted_iota(jnp.int32, lengths.shape, 0)
    place = lax.broadcasted_iota(jnp.int32, (GROUP, LANES), 0)
    keeps = jnp.ones(keep.shape, jnp.float32)
    sizes = jnp.zeros(lengths.shape, jnp.float32)
    first = jnp.int32(0)
    for d in range(docs):
        count = counts[d]
        full = count // GROUP
        inside[d * GROUP : (d + 1) * GROUP, :] = (place < count - full * GROUP).astype(jnp.float32)
        keeps = jnp.where(group == jnp.where(full > 0, first, groups), 0.0, keeps)
        sizes = jnp.where(document == d, count.astype(jnp.float32), sizes)
        first = first + full
    keep[...] = keeps
    first = jnp.int32(0)
    for d in range(docs):
        full = counts[d] // GROUP
        last[d] = jnp.where(full > 0, first + full - 1, groups)
        first = first + full
    last[docs] = first
    lengths[...] = sizes


def document_layout(counts, rows):
    docs, groups = counts.shape[0], rows // GROUP
    return pl.pallas_call(
        layout_kernel,
        out_shape=(
            jax.ShapeDtypeStruct((docs * GROUP, LANES), jnp.float32),
            jax.ShapeDtypeStruct((groups, LANES), jnp.float32),
            pltpu.SMEM((docs + 1,), jnp.int32),
            jax.ShapeDtypeStruct((docs, LANES), jnp.float32),
        ),
        in_specs=[ANY],
        out_specs=(VMEM, VMEM, SMEM, VMEM),
        scratch_shapes=[pltpu.SMEM((docs,), jnp.int32), pltpu.SemaphoreType.DMA],
        compiler_params=params(4),
        cost_estimate=cost(20000),
        name="layout",
    )(pltpu.with_memory_space_constraint(counts, pltpu.HBM))


def docs_kernel(counts_any, hidden, w_proj, rows_out, vectors, counts, sem):
    docs = counts.shape[0]
    rows = hidden.shape[0]
    tail = docs * GROUP
    fetch = pltpu.make_async_copy(counts_any, counts, sem)
    fetch.start()
    step = 384 if rows % 384 == 0 else rows
    for lo in range(0, rows, step):
        block = slice(lo, lo + step)
        projected = jnp.dot(hidden[block, :], w_proj[...], preferred_element_type=jnp.float32)
        vectors[block, :] = unit_rows(projected).astype(jnp.float32)
    vectors[rows:, :] = jnp.zeros_like(vectors[rows:, :])
    rows_out[tail:, :] = jnp.zeros_like(rows_out[tail:, :])
    fetch.wait()
    start = jnp.int32(0)
    first = jnp.int32(0)
    for d in range(docs):
        count = counts[d]
        full = count // GROUP

        def move(k, carry, start=start, first=first):
            block = vectors[pl.ds(start + k * BLOCK, BLOCK), :]
            at = pl.multiple_of(tail + first * GROUP + k * BLOCK, GROUP)
            rows_out[pl.ds(at, BLOCK), :] = block.astype(jnp.bfloat16)
            return carry

        lax.fori_loop(0, (full * GROUP + BLOCK - 1) // BLOCK, move, 0)
        block = vectors[pl.ds(start + full * GROUP, GROUP), :]
        rows_out[d * GROUP : (d + 1) * GROUP, :] = block.astype(jnp.bfloat16)
        start = start + count
        first = first + full


def regroup_documents(hidden, counts, w_proj):
    rows, docs = hidden.shape[0], counts.shape[0]
    width = w_proj.shape[1]
    return pl.pallas_call(
        docs_kernel,
        out_shape=jax.ShapeDtypeStruct((docs * GROUP + rows + BLOCK, width), jnp.bfloat16),
        in_specs=[ANY, VMEM, VMEM],
        out_specs=VMEM,
        scratch_shapes=[
            pltpu.VMEM((rows + BLOCK, width), jnp.float32),
            pltpu.SMEM((docs,), jnp.int32),
            pltpu.SemaphoreType.DMA,
        ],
        compiler_params=params(16),
        cost_estimate=cost(2.5),
        name="documents",
    )(pltpu.with_memory_space_constraint(counts, pltpu.HBM), hidden, w_proj)


def unit_kernel(*refs):
    *pieces, out = refs
    for i, piece in enumerate(pieces):
        values = piece[...].reshape(PIECE, piece.shape[-1])
        out[i * PIECE : (i + 1) * PIECE, :] = unit_rows(values)


def unit_pieces(*pieces):
    return pl.pallas_call(
        unit_kernel,
        out_shape=jax.ShapeDtypeStruct((len(pieces) * PIECE, pieces[0].shape[-1]), jnp.bfloat16),
        in_specs=[VMEM] * len(pieces),
        out_specs=VMEM,
        compiler_params=params(8),
        cost_estimate=cost(0.2),
        name="unit_pieces",
    )(*pieces)


def mass_kernel(places, rows, inside, keep, last, *refs):
    *chunks, mass, sums, tail_sums = refs
    chunks = chunks[-len(places) :]
    docs = last.shape[0] - 1
    groups = keep.shape[0]
    tail = docs * GROUP

    def weights(block, tokens):
        sims = lax.dot_general(
            block, tokens, (((1,), (1,)), ((), ())), preferred_element_type=jnp.float32
        )
        return jnp.exp2(sims * (BETA * LOG2E))

    def wide(row, width):
        return jnp.concatenate([row] * (width // LANES), axis=1)

    used = last[docs]
    for c, chunk in enumerate(chunks):
        width = chunk.shape[0]
        sums[c, groups] = jnp.zeros((HALF, width), jnp.float32)

    def run(size):
        for c, chunk in enumerate(chunks):
            tokens = chunk[...]
            width = tokens.shape[0]
            block = weights(rows[:tail, :], tokens)
            for d in range(docs):
                lo = d * GROUP
                mid, hi = lo + HALF, lo + GROUP
                tail_sums[c, d] = block[lo:mid] * wide(inside[lo:mid, :], width) + block[
                    mid:hi
                ] * wide(inside[mid:hi, :], width)
            total = jnp.zeros((HALF, width), jnp.float32)
            for base in range(0, size, STEP):
                step = min(STEP, size - base)
                block = weights(rows[tail + base * GROUP : tail + (base + step) * GROUP, :], tokens)
                for j in range(step):
                    lo = j * GROUP
                    mid, hi = lo + HALF, lo + GROUP
                    row = jnp.broadcast_to(keep[base + j : base + j + 1, :], (HALF, LANES))
                    total = total * wide(row, width) + (block[lo:mid] + block[mid:hi])
                    sums[c, base + j] = total

    sizes = [size for size in SIZES if size < groups] + [groups]
    for below, size in zip([-1] + sizes, sizes):
        pl.when((used > below) & (used <= size))(functools.partial(run, size))
    odd = lax.axis_index("loop") % 2
    for c, place in enumerate(places):
        at = [even if even == other else jnp.where(odd == 0, even, other) for even, other in place]
        for d in range(docs):
            total = jnp.sum(sums[c, last[d]] + tail_sums[c, d], axis=0, keepdims=True)
            for i, piece in enumerate(at):
                mass[piece, d : d + 1, :] = total[:, i * PIECE : (i + 1) * PIECE]


def add_masses(documents, mass, chunks, places, pieces):
    rows, inside, keep, last, _ = documents
    docs, groups = last.shape[0] - 1, keep.shape[0]
    last = pltpu.with_memory_space_constraint(last, pltpu.SMEM)
    count, width = len(chunks), chunks[0].shape[0]
    before = () if mass is None else (mass,)
    return pl.pallas_call(
        functools.partial(mass_kernel, places),
        out_shape=jax.ShapeDtypeStruct((pieces, docs, PIECE), jnp.float32),
        in_specs=[VMEM, VMEM, VMEM, SMEM] + [VMEM] * (len(before) + count),
        out_specs=VMEM,
        input_output_aliases={4: 0} if before else {},
        scratch_shapes=[
            pltpu.VMEM((count, groups + 1, HALF, width), jnp.float32),
            pltpu.VMEM((count, docs, HALF, width), jnp.float32),
        ],
        compiler_params=params(28),
        cost_estimate=cost(20000),
        name="masses",
    )(rows, inside, keep, last, *before, *chunks)


def score_kernel(parts, tokens, relative, lengths, mass, scores):
    pieces, docs, _ = mass.shape
    groups = pieces // parts
    queries = PIECE // tokens
    per_tile = LANES // queries
    tiles = groups // per_tile
    own = lax.axis_index("loop") if relative else 0
    sizes = jnp.concatenate([lengths[...]] * (PIECE // LANES), axis=1)
    place = lax.broadcasted_iota(jnp.int32, (PIECE, LANES), 0) // tokens
    column = lax.broadcasted_iota(jnp.int32, (PIECE, LANES), 1)
    total = jnp.zeros((tiles * docs, LANES), jnp.float32)
    for i in range(per_tile):
        logs = []
        for tile in range(tiles):
            at = ((tile * per_tile + i) ^ own) * parts
            logs.append(sum(jnp.log(mass[at + part] / sizes) for part in range(parts)))
        rest = jnp.concatenate(logs, axis=0)
        pick = (column == place + i * queries).astype(jnp.bfloat16)
        for _ in range(3):
            head = rest.astype(jnp.bfloat16)
            total = total + jnp.dot(head, pick, preferred_element_type=jnp.float32)
            rest = rest - head.astype(jnp.float32)
    total = total * (1.0 / (tokens * parts))
    for tile in range(tiles):
        scores[:, tile * LANES : (tile + 1) * LANES] = total[tile * docs : (tile + 1) * docs]


def score(parts, tokens, relative, lengths, mass):
    pieces, docs, _ = mass.shape
    queries = pieces // parts * (PIECE // tokens)
    return pl.pallas_call(
        functools.partial(score_kernel, parts, tokens, relative),
        out_shape=jax.ShapeDtypeStruct((docs, queries), jnp.float32),
        in_specs=[VMEM, VMEM],
        out_specs=VMEM,
        compiler_params=params(8),
        cost_estimate=cost(1),
        name="scores",
    )(lengths, mass)


def swap(values, even, odd=None):
    odd = even if odd is None else odd
    pairs = [(i, i ^ (even if i % 2 == 0 else odd)) for i in range(32)]
    return lax.ppermute(values, ("shard", "loop"), pairs)


def pair_body(hidden, segment, counts, w_proj, seeds):
    devices = 32
    core, x, z, far, y = 1, 2, 4, 8, 16
    after = lax.optimization_barrier
    raw_far = swap(seeds, far, x)
    raw_z = swap(seeds, z, y)
    layout = document_layout(counts, hidden.shape[0])
    raw_far, layout = after((raw_far, layout))
    raw_both = swap(raw_far, z, y)
    near = unit_pieces(seeds, raw_z)
    first_near = swap(near, x, far)
    away = unit_pieces(raw_far, raw_both)
    first_away = swap(away, x, far)
    own = jnp.concatenate([near, away], axis=0)
    own_core = swap(own, core)
    hidden, away = after((hidden, away))
    rows = regroup_documents(hidden, counts, w_proj)
    documents = (rows, *layout)

    def add(mass, chunk, masks, through_core):
        lanes = [
            [mask ^ bits for bits in (0, one, two, one | two)]
            for mask, one, two in ((masks[0], z, far), (masks[1], y, x))
        ]
        if through_core:
            lanes = [[mask ^ core for mask in lane] for lane in lanes[::-1]]
        place = tuple(
            tuple((mask & 15) * 2 + (mask >> 4) for mask in pair) for pair in zip(*lanes)
        )
        return add_masses(documents, mass, (chunk,), (place,), devices)

    mass = add(None, own, (0, 0), False)
    first_near, first_away, own, mass = after((first_near, first_away, own, mass))
    first = jnp.concatenate([first_near, first_away], axis=0)
    third = swap(first, y, z)
    second = swap(own, y, z)
    mass = add(mass, own_core, (0, 0), True)
    first, mass = after((first, mass))
    first_core = swap(first, core)
    mass = add(mass, first, (x, far), False)
    mass = add(mass, first_core, (x, far), True)
    third, mass = after((third, mass))
    third_core = swap(third, core)
    mass = add(mass, third, (x | y, z | far), False)
    mass = add(mass, third_core, (x | y, z | far), True)
    second, mass = after((second, mass))
    second_core = swap(second, core)
    mass = add(mass, second, (y, z), False)
    mass = add(mass, second_core, (y, z), True)
    return score(2, 16, True, documents[-1], mass)


def whole_body(hidden, segment, counts, w_proj, seeds):
    own = lax.all_gather(unit_rows(seeds), "shard", axis=1, tiled=True)
    every = lax.all_gather(own, "loop", axis=0, tiled=True)
    tokens = every.shape[1]
    every = every.reshape(-1, every.shape[-1])
    pieces = every.shape[0] // PIECE
    layout = document_layout(counts, hidden.shape[0])
    documents = (regroup_documents(hidden, counts, w_proj), *layout)
    mass = None
    for first in range(0, pieces, 4):
        places = (tuple((piece, piece) for piece in range(first, first + 4)),)
        chunk = every[first * PIECE : (first + 4) * PIECE]
        mass = add_masses(documents, mass, (chunk,), places, pieces)
    return score(1, tokens, False, documents[-1], mass)


def solution(mesh):
    in_specs = (
        P(("shard", "loop"), None),
        P(("shard", "loop")),
        P(("shard", "loop")),
        P(),
        P("loop", "shard", None),
    )
    out_specs = P(("shard", "loop"), None)
    paired = mesh.shape["shard"] == 2 and mesh.shape["loop"] == 16
    body = pair_body if paired else whole_body
    return jax.shard_map(body, mesh=mesh, in_specs=in_specs, out_specs=out_specs, check_vma=False)
```

```python
import functools

import jax
import jax.numpy as jnp
from jax import lax
from jax.experimental import pallas as pl
from jax.experimental.pallas import tpu as pltpu
from jax.sharding import PartitionSpec as P

BETA = 16.0
EPS = 1e-06
LOG2E = 1.4426950408889634
GROUP = 16
HALF = GROUP // 2
PIECE = 256
LANES = 128
STEP = 24
SIZES = (84, 100)
BLOCK = 64
ANY = pl.BlockSpec(memory_space=pl.ANY)
VMEM = pl.BlockSpec(memory_space=pltpu.VMEM)
SMEM = pl.BlockSpec(memory_space=pltpu.SMEM)


def unit_rows(values):
    values = values.astype(jnp.float32)
    return (values * lax.rsqrt(jnp.sum(values * values, axis=-1, keepdims=True) + EPS)).astype(
        jnp.bfloat16
    )


def params(mib):
    return pltpu.CompilerParams(vmem_limit_bytes=mib * 2**20)


def cost(micros):
    return pl.CostEstimate(flops=int(micros * 1e6), bytes_accessed=0, transcendentals=0)


def layout_kernel(counts_any, inside, keep, last, lengths, counts, sem):
    docs, groups = counts.shape[0], keep.shape[0]
    fetch = pltpu.make_async_copy(counts_any, counts, sem)
    fetch.start()
    fetch.wait()
    group = lax.broadcasted_iota(jnp.int32, keep.shape, 0)
    document = lax.broadcasted_iota(jnp.int32, lengths.shape, 0)
    place = lax.broadcasted_iota(jnp.int32, (GROUP, LANES), 0)
    keeps = jnp.ones(keep.shape, jnp.float32)
    sizes = jnp.zeros(lengths.shape, jnp.float32)
    first = jnp.int32(0)
    for d in range(docs):
        count = counts[d]
        full = count // GROUP
        inside[d * GROUP : (d + 1) * GROUP, :] = (place < count - full * GROUP).astype(jnp.float32)
        keeps = jnp.where(group == jnp.where(full > 0, first, groups), 0.0, keeps)
        sizes = jnp.where(document == d, count.astype(jnp.float32), sizes)
        first = first + full
    keep[...] = keeps
    first = jnp.int32(0)
    for d in range(docs):
        full = counts[d] // GROUP
        last[d] = jnp.where(full > 0, first + full - 1, groups)
        first = first + full
    last[docs] = first
    lengths[...] = sizes


def document_layout(counts, rows):
    docs, groups = counts.shape[0], rows // GROUP
    return pl.pallas_call(
        layout_kernel,
        out_shape=(
            jax.ShapeDtypeStruct((docs * GROUP, LANES), jnp.float32),
            jax.ShapeDtypeStruct((groups, LANES), jnp.float32),
            pltpu.SMEM((docs + 1,), jnp.int32),
            jax.ShapeDtypeStruct((docs, LANES), jnp.float32),
        ),
        in_specs=[ANY],
        out_specs=(VMEM, VMEM, SMEM, VMEM),
        scratch_shapes=[pltpu.SMEM((docs,), jnp.int32), pltpu.SemaphoreType.DMA],
        compiler_params=params(4),
        cost_estimate=cost(20000),
        name="layout",
    )(pltpu.with_memory_space_constraint(counts, pltpu.HBM))


def docs_kernel(counts_any, hidden, w_proj, rows_out, vectors, counts, sem):
    docs = counts.shape[0]
    rows = hidden.shape[0]
    tail = docs * GROUP
    fetch = pltpu.make_async_copy(counts_any, counts, sem)
    fetch.start()
    step = 384 if rows % 384 == 0 else rows
    for lo in range(0, rows, step):
        block = slice(lo, lo + step)
        projected = jnp.dot(hidden[block, :], w_proj[...], preferred_element_type=jnp.float32)
        vectors[block, :] = unit_rows(projected).astype(jnp.float32)
    vectors[rows:, :] = jnp.zeros_like(vectors[rows:, :])
    rows_out[tail:, :] = jnp.zeros_like(rows_out[tail:, :])
    fetch.wait()
    start = jnp.int32(0)
    first = jnp.int32(0)
    for d in range(docs):
        count = counts[d]
        full = count // GROUP

        def move(k, carry, start=start, first=first):
            block = vectors[pl.ds(start + k * BLOCK, BLOCK), :]
            at = pl.multiple_of(tail + first * GROUP + k * BLOCK, GROUP)
            rows_out[pl.ds(at, BLOCK), :] = block.astype(jnp.bfloat16)
            return carry

        lax.fori_loop(0, (full * GROUP + BLOCK - 1) // BLOCK, move, 0)
        block = vectors[pl.ds(start + full * GROUP, GROUP), :]
        rows_out[d * GROUP : (d + 1) * GROUP, :] = block.astype(jnp.bfloat16)
        start = start + count
        first = first + full


def regroup_documents(hidden, counts, w_proj):
    rows, docs = hidden.shape[0], counts.shape[0]
    width = w_proj.shape[1]
    return pl.pallas_call(
        docs_kernel,
        out_shape=jax.ShapeDtypeStruct((docs * GROUP + rows + BLOCK, width), jnp.bfloat16),
        in_specs=[ANY, VMEM, VMEM],
        out_specs=VMEM,
        scratch_shapes=[
            pltpu.VMEM((rows + BLOCK, width), jnp.float32),
            pltpu.SMEM((docs,), jnp.int32),
            pltpu.SemaphoreType.DMA,
        ],
        compiler_params=params(16),
        cost_estimate=cost(2.5),
        name="documents",
    )(pltpu.with_memory_space_constraint(counts, pltpu.HBM), hidden, w_proj)


def unit_kernel(*refs):
    *pieces, out = refs
    for i, piece in enumerate(pieces):
        values = piece[...].reshape(PIECE, piece.shape[-1])
        out[i * PIECE : (i + 1) * PIECE, :] = unit_rows(values)


def unit_pieces(*pieces):
    return pl.pallas_call(
        unit_kernel,
        out_shape=jax.ShapeDtypeStruct((len(pieces) * PIECE, pieces[0].shape[-1]), jnp.bfloat16),
        in_specs=[VMEM] * len(pieces),
        out_specs=VMEM,
        compiler_params=params(8),
        cost_estimate=cost(0.2),
        name="unit_pieces",
    )(*pieces)


def mass_kernel(places, rows, inside, keep, last, *refs):
    *chunks, mass, sums, tail_sums = refs
    chunks = chunks[-len(places) :]
    docs = last.shape[0] - 1
    groups = keep.shape[0]
    tail = docs * GROUP

    def weights(block, tokens):
        sims = lax.dot_general(
            block, tokens, (((1,), (1,)), ((), ())), preferred_element_type=jnp.float32
        )
        return jnp.exp2(sims * (BETA * LOG2E))

    def wide(row, width):
        return jnp.concatenate([row] * (width // LANES), axis=1)

    used = last[docs]
    for c, chunk in enumerate(chunks):
        width = chunk.shape[0]
        sums[c, groups] = jnp.zeros((HALF, width), jnp.float32)

    def run(size):
        for c, chunk in enumerate(chunks):
            tokens = chunk[...]
            width = tokens.shape[0]
            block = weights(rows[:tail, :], tokens)
            for d in range(docs):
                lo = d * GROUP
                mid, hi = lo + HALF, lo + GROUP
                tail_sums[c, d] = block[lo:mid] * wide(inside[lo:mid, :], width) + block[
                    mid:hi
                ] * wide(inside[mid:hi, :], width)
            total = jnp.zeros((HALF, width), jnp.float32)
            for base in range(0, size, STEP):
                step = min(STEP, size - base)
                block = weights(rows[tail + base * GROUP : tail + (base + step) * GROUP, :], tokens)
                for j in range(step):
                    lo = j * GROUP
                    mid, hi = lo + HALF, lo + GROUP
                    row = jnp.broadcast_to(keep[base + j : base + j + 1, :], (HALF, LANES))
                    total = total * wide(row, width) + (block[lo:mid] + block[mid:hi])
                    sums[c, base + j] = total

    sizes = [size for size in SIZES if size < groups] + [groups]
    for below, size in zip([-1] + sizes, sizes):
        pl.when((used > below) & (used <= size))(functools.partial(run, size))
    odd = lax.axis_index("loop") % 2
    for c, place in enumerate(places):
        at = [even if even == other else jnp.where(odd == 0, even, other) for even, other in place]
        for d in range(docs):
            total = jnp.sum(sums[c, last[d]] + tail_sums[c, d], axis=0, keepdims=True)
            for i, piece in enumerate(at):
                mass[piece, d : d + 1, :] = total[:, i * PIECE : (i + 1) * PIECE]


def add_masses(documents, mass, chunks, places, pieces):
    rows, inside, keep, last, _ = documents
    docs, groups = last.shape[0] - 1, keep.shape[0]
    last = pltpu.with_memory_space_constraint(last, pltpu.SMEM)
    count, width = len(chunks), chunks[0].shape[0]
    before = () if mass is None else (mass,)
    return pl.pallas_call(
        functools.partial(mass_kernel, places),
        out_shape=jax.ShapeDtypeStruct((pieces, docs, PIECE), jnp.float32),
        in_specs=[VMEM, VMEM, VMEM, SMEM] + [VMEM] * (len(before) + count),
        out_specs=VMEM,
        input_output_aliases={4: 0} if before else {},
        scratch_shapes=[
            pltpu.VMEM((count, groups + 1, HALF, width), jnp.float32),
            pltpu.VMEM((count, docs, HALF, width), jnp.float32),
        ],
        compiler_params=params(28),
        cost_estimate=cost(20000),
        name="masses",
    )(rows, inside, keep, last, *before, *chunks)


def score_kernel(parts, tokens, relative, lengths, mass, scores):
    pieces, docs, _ = mass.shape
    groups = pieces // parts
    queries = PIECE // tokens
    per_tile = LANES // queries
    tiles = groups // per_tile
    own = lax.axis_index("loop") if relative else 0
    sizes = jnp.concatenate([lengths[...]] * (PIECE // LANES), axis=1)
    place = lax.broadcasted_iota(jnp.int32, (PIECE, LANES), 0) // tokens
    column = lax.broadcasted_iota(jnp.int32, (PIECE, LANES), 1)
    total = jnp.zeros((tiles * docs, LANES), jnp.float32)
    for i in range(per_tile):
        logs = []
        for tile in range(tiles):
            at = ((tile * per_tile + i) ^ own) * parts
            ratio = mass[at] / sizes
            for part in range(1, parts):
                ratio = ratio * (mass[at + part] / sizes)
            logs.append(jnp.log(ratio))
        rest = jnp.concatenate(logs, axis=0)
        pick = (column == place + i * queries).astype(jnp.bfloat16)
        for _ in range(2):
            head = rest.astype(jnp.bfloat16)
            total = total + jnp.dot(head, pick, preferred_element_type=jnp.float32)
            rest = rest - head.astype(jnp.float32)
    total = total * (1.0 / (tokens * parts))
    for tile in range(tiles):
        scores[:, tile * LANES : (tile + 1) * LANES] = total[tile * docs : (tile + 1) * docs]


def score(parts, tokens, relative, lengths, mass):
    pieces, docs, _ = mass.shape
    queries = pieces // parts * (PIECE // tokens)
    return pl.pallas_call(
        functools.partial(score_kernel, parts, tokens, relative),
        out_shape=jax.ShapeDtypeStruct((docs, queries), jnp.float32),
        in_specs=[VMEM, VMEM],
        out_specs=VMEM,
        compiler_params=params(8),
        cost_estimate=cost(1),
        name="scores",
    )(lengths, mass)


def swap(values, even, odd=None):
    odd = even if odd is None else odd
    pairs = [(i, i ^ (even if i % 2 == 0 else odd)) for i in range(32)]
    return lax.ppermute(values, ("shard", "loop"), pairs)


def pair_body(hidden, segment, counts, w_proj, seeds):
    devices = 32
    core, x, z, far, y = 1, 2, 4, 8, 16
    after = lax.optimization_barrier
    raw_far = swap(seeds, far, x)
    raw_z = swap(seeds, z, y)
    layout = document_layout(counts, hidden.shape[0])
    raw_far, layout = after((raw_far, layout))
    raw_both = swap(raw_far, z, y)
    near = unit_pieces(seeds, raw_z)
    first_near = swap(near, x, far)
    away = unit_pieces(raw_far, raw_both)
    first_away = swap(away, x, far)
    own = jnp.concatenate([near, away], axis=0)
    own_core = swap(own, core)
    hidden, away = after((hidden, away))
    rows = regroup_documents(hidden, counts, w_proj)
    documents = (rows, *layout)

    def add(mass, chunk, masks, through_core):
        lanes = [
            [mask ^ bits for bits in (0, one, two, one | two)]
            for mask, one, two in ((masks[0], z, far), (masks[1], y, x))
        ]
        if through_core:
            lanes = [[mask ^ core for mask in lane] for lane in lanes[::-1]]
        place = tuple(
            tuple((mask & 15) * 2 + (mask >> 4) for mask in pair) for pair in zip(*lanes)
        )
        return add_masses(documents, mass, (chunk,), (place,), devices)

    mass = add(None, own, (0, 0), False)
    first_near, first_away, own, mass = after((first_near, first_away, own, mass))
    first = jnp.concatenate([first_near, first_away], axis=0)
    third = swap(first, y, z)
    second = swap(own, y, z)
    mass = add(mass, own_core, (0, 0), True)
    first, mass = after((first, mass))
    first_core = swap(first, core)
    mass = add(mass, first, (x, far), False)
    mass = add(mass, first_core, (x, far), True)
    third, mass = after((third, mass))
    third_core = swap(third, core)
    mass = add(mass, third, (x | y, z | far), False)
    mass = add(mass, third_core, (x | y, z | far), True)
    second, mass = after((second, mass))
    second_core = swap(second, core)
    mass = add(mass, second, (y, z), False)
    mass = add(mass, second_core, (y, z), True)
    return score(2, 16, True, documents[-1], mass)


def whole_body(hidden, segment, counts, w_proj, seeds):
    own = lax.all_gather(unit_rows(seeds), "shard", axis=1, tiled=True)
    every = lax.all_gather(own, "loop", axis=0, tiled=True)
    tokens = every.shape[1]
    every = every.reshape(-1, every.shape[-1])
    pieces = every.shape[0] // PIECE
    layout = document_layout(counts, hidden.shape[0])
    documents = (regroup_documents(hidden, counts, w_proj), *layout)
    mass = None
    for first in range(0, pieces, 4):
        places = (tuple((piece, piece) for piece in range(first, first + 4)),)
        chunk = every[first * PIECE : (first + 4) * PIECE]
        mass = add_masses(documents, mass, (chunk,), places, pieces)
    return score(1, tokens, False, documents[-1], mass)


def solution(mesh):
    in_specs = (
        P(("shard", "loop"), None),
        P(("shard", "loop")),
        P(("shard", "loop")),
        P(),
        P("loop", "shard", None),
    )
    out_specs = P(("shard", "loop"), None)
    paired = mesh.shape["shard"] == 2 and mesh.shape["loop"] == 16
    body = pair_body if paired else whole_body
    return jax.shard_map(body, mesh=mesh, in_specs=in_specs, out_specs=out_specs, check_vma=False)
```
